32 devices in a mesh: kv: 4 (over x, core), seq: 4 (over z), exp: 2 (over y).
Axes of the slice: x: 2, y: 2, z: 4, core: 2. Of those that a mesh axis runs over, the one named last changes fastest.
Arguments:
- queries: bfloat16 [16, 64, 2048], P(('kv', 'seq')), may hold values from -8 to 8
- draft_kv: bfloat16 [2, 16, 64, 2048], P(None, ('kv', 'seq'), 'exp'), may hold values from -12 to 12
- kv_pool: bfloat16 [2, 384, 16, 2048], P(None, ('kv', 'seq', 'exp')), may hold values from -12 to 12
- page_table: int32 [16, 12, 2], P(('kv', 'seq'), None, 'exp'), may hold values from 0 to 11, as said below
- cache_lens: int32 [16], P(('kv', 'seq')), may hold values from 1 to 384, as said below
- parents: int32 [16, 64], P(('kv', 'seq')), may hold values from -1 to 62, as said below
- hidden: bfloat16 [16, 64, 2048], P(('kv', 'seq')), may hold values from -36 to 36
- norm_gain: bfloat16 [2048], replicated, may hold values from 0.5 to 1.5
- out_proj: bfloat16 [2048, 2048], P('exp'), may hold values from -0.125 to 0.125
- router: bfloat16 [2048, 64], replicated, may hold values from -0.125 to 0.125
- routes: int32 [16, 64, 8], P(('kv', 'seq')), may hold values from 0 to 63, all different within a row; in each aligned block of 64 rows (0 to 63, 64 to 127, ..., all dimensions but the last counted through in order) at most 16 rows name the same one
- gate_w: bfloat16 [64, 2048, 1024], P(('kv', 'seq'), None, 'exp'), may hold values from -0.125 to 0.125
- up_w: bfloat16 [64, 2048, 1024], P(('kv', 'seq'), None, 'exp'), may hold values from -0.125 to 0.125
- down_w: bfloat16 [64, 1024, 2048], P(('kv', 'seq'), 'exp'), may hold values from -0.1875 to 0.1875
Outputs:
- output: bfloat16 [16, 64, 2048], P(('kv', 'seq'), None, 'exp')
The draws below stay inside these ranges and needn't reach their ends.
Inputs may be any that keep to these rules, and one draw needn't show every extreme that they name: For one block of 1 request and one page set s, the entries page_table[r, j, s] over the block's requests r and all j are a permutation of 0 .. 11. `cache_lens`: some request has exactly 384 cached positions. parents[r, 0] = -1; for i >= 1, parents[r, i] is an earlier draft position. `routes`: in each aligned block of 64 token rows (the rows of one device, requests in order), no expert is named by more than 16 rows.
All inputs are finite; a program needn't handle non-finite values.
Results may differ from the reference program's by a relative error of at most 0.02.
Values may be sent and summed in bfloat16 or wider, within the bound.
A program may use at most 128 MiB of HBM per device.

```python
import math
import jax
import jax.numpy as jnp
import numpy as np
from jax import lax

D = 2048
H = 16
HD = 128
FF = 1024
EXPERTS = 64
TOPK = 8
DRAFT = 64
PAGE = 16
RK = 1
PPD = 12
SETS = 2
REQS = 16
MAXLEN = 384
POOL = 384
CAP = 16


def draw_queries(key, part):
    array_shape = (REQS, DRAFT, H * HD)
    noise_key = jax.random.fold_in(key, 101)
    values = jnp.clip(jax.random.normal(noise_key, array_shape, jnp.float32), -6.0, 6.0)
    return values.astype(jnp.bfloat16)


def draw_draft_kv(key, part):
    array_shape = (REQS, DRAFT, H * HD)
    key_noise = jax.random.fold_in(key, 201)
    value_noise = jax.random.fold_in(key, 202)
    key_rows = 2.5 * jnp.clip(jax.random.normal(key_noise, array_shape, jnp.float32), -4.0, 4.0)
    value_rows = jnp.clip(jax.random.normal(value_noise, array_shape, jnp.float32), -6.0, 6.0)
    return jnp.stack([key_rows, value_rows]).astype(jnp.bfloat16)


def draw_kv_pool(key, part):
    array_shape = (POOL, PAGE, H * HD)
    key_noise = jax.random.fold_in(key, 301)
    value_noise = jax.random.fold_in(key, 302)
    key_rows = 2.5 * jnp.clip(jax.random.normal(key_noise, array_shape, jnp.float32), -4.0, 4.0)
    value_rows = jnp.clip(jax.random.normal(value_noise, array_shape, jnp.float32), -6.0, 6.0)
    return jnp.stack([key_rows, value_rows]).astype(jnp.bfloat16)


def draw_page_table(key, part):
    blocks = REQS // RK
    key_list = jax.random.split(jax.random.fold_in(key, 351), blocks * SETS)
    orders = jax.vmap(lambda single_key: jax.random.permutation(single_key, RK * PPD))(key_list)
    orders = orders.reshape(blocks, SETS, RK, PPD)
    return jnp.transpose(orders, (0, 2, 3, 1)).reshape(REQS, PPD, SETS).astype(jnp.int32)


def draw_cache_lens(key, part):
    first_draw = jax.random.randint(jax.random.fold_in(key, 401), (REQS,), 1, MAXLEN + 1)
    second_draw = jax.random.randint(jax.random.fold_in(key, 402), (REQS,), 1, MAXLEN + 1)
    longest = jax.random.randint(jax.random.fold_in(key, 403), (), 0, REQS)
    lengths = jnp.minimum(first_draw, second_draw)
    return jnp.where(jnp.arange(REQS, dtype=jnp.int32) == longest, MAXLEN, lengths).astype(jnp.int32)


def draw_parents(key, part):
    raw_bits = jax.random.randint(jax.random.fold_in(key, 451), (REQS, DRAFT), 0, 1 << 20)
    position = jnp.arange(DRAFT, dtype=jnp.int32)[None, :]
    lowest = jnp.maximum(position - 4, 0)
    spread = jnp.maximum(position - lowest, 1)
    linked = jnp.where(position == DRAFT - 1, DRAFT - 2, lowest + raw_bits % spread)
    return jnp.where(position == 0, -1, linked).astype(jnp.int32)


def draw_hidden(key, part):
    row_scale = jnp.exp(jax.random.uniform(jax.random.fold_in(key, 501), (REQS, DRAFT, 1), jnp.float32, math.log(0.3), math.log(3.0)))
    column_scale = jnp.exp(jax.random.uniform(jax.random.fold_in(key, 502), (1, 1, D), jnp.float32, math.log(0.3), math.log(3.0)))
    noise_key = jax.random.fold_in(key, 503)
    drawn_rows = jnp.clip(jax.random.normal(noise_key, (REQS, DRAFT, D), jnp.float32), -4.0, 4.0)
    return (drawn_rows * row_scale * column_scale).astype(jnp.bfloat16)


def level_of(key, shape, cuts, low, largest):
    factor_of = 1.0
    for dim, blocks in cuts:
        steps = jax.random.uniform(jax.random.fold_in(jax.random.fold_in(key, 6), dim), (blocks,), jnp.float32, low / len(cuts), largest / len(cuts))
        factor_of = factor_of * jnp.repeat(jnp.exp(steps), shape[dim] // blocks).reshape((-1,) + (1,) * (len(shape) - 1 - dim))
    return factor_of


def routed_block(key, own, number, rows, count, top, bound, skew):
    ranking = jax.random.permutation(key, count)
    crowded, ordinary = shares(count, rows * top, bound, skew, True), shares(count, rows * top, bound, skew, False)
    places = jnp.arange(count)

    def named(tallies, turn):
        used = int((tallies > 0).sum())
        fixed = max(1, used // 4)
        shifted = fixed + (places - fixed + turn * (used - fixed)) % max(1, count - fixed)
        return jnp.zeros((count,), jnp.int32).at[ranking[jnp.where(places < fixed, places, shifted)]].set(jnp.asarray(tallies, jnp.int32))

    tallies = jnp.where(number % 4 == 0, named(crowded, number // 4), named(ordinary, number - number // 4 - 1))
    mixed = jax.random.permutation(jax.random.fold_in(own, 3), count)
    donor, receiver = mixed[0:count // 2 * 2:2], mixed[1:count // 2 * 2:2]
    slack = jnp.minimum(tallies[donor] - 1, bound - tallies[receiver]) // 2
    slack = jnp.where((donor == ranking[0]) | (receiver == ranking[0]) | (tallies[receiver] == 0), 0, jnp.maximum(slack, 0))
    shifted = jax.random.randint(jax.random.fold_in(own, 4), (count // 2,), 0, 1 << 20) % (slack + 1)
    tallies = tallies.at[donor].add(-shifted).at[receiver].add(shifted)
    items = jnp.searchsorted(jnp.cumsum(tallies), jnp.arange(rows * top), side="right").astype(jnp.int32)
    listing = items.reshape(top, rows).T
    listing = listing[jax.random.permutation(jax.random.fold_in(own, 1), rows)]
    turn = jax.random.randint(jax.random.fold_in(own, 2), (rows, 1), 0, top)
    return jnp.take_along_axis(listing, (jnp.arange(top)[None, :] + turn) % top, axis=1)


def shares(number_of, total, bound, lean, full):
    weights = [(1 << 20) // math.isqrt(rank ** lean) + 1 for rank in range(1, number_of + 1)]
    largest = bound if full else min(bound, max(-(-total // number_of), total * weights[0] // sum(weights)))
    least = 1 if total - largest >= number_of - 1 else 0
    given, surplus = [largest] + [least] * (number_of - 1), total - largest - least * (number_of - 1)
    while surplus > 0:
        free = [i for i in range(1, number_of) if given[i] < largest] or [i for i in range(1, number_of) if given[i] < bound]
        whole, remaining = sum([weights[i] for i in free]), surplus
        for i in free:
            more = min(bound - given[i], max(1, remaining * weights[i] // whole), surplus)
            given[i] = given[i] + more
            surplus = surplus - more
    return np.array(given)


def bell_draw(own_key, shape, scale, bound, pieces=(), held_as=jnp.bfloat16):
    factor_of = level_of(own_key, shape, pieces, -0.22, 0.18) if pieces else 1.0
    array = jax.random.normal(own_key, shape, jnp.float32) * scale * factor_of
    return jnp.minimum(jnp.maximum(array, -bound), bound).astype(held_as)


def setup_inputs(seed: int = 0) -> dict:
    splits = jax.random.split(jax.random.key(seed), 15)
    queries = draw_queries(jax.random.fold_in(splits[14], 71), 0)
    draft_kv = draw_draft_kv(jax.random.fold_in(splits[14], 71), 0)
    kv_pool = draw_kv_pool(jax.random.fold_in(splits[14], 71), 0)
    page_table = draw_page_table(jax.random.fold_in(splits[14], 71), 0)
    cache_lens = draw_cache_lens(jax.random.fold_in(splits[14], 71), 0)
    parents = draw_parents(jax.random.fold_in(splits[14], 71), 0)
    hidden = draw_hidden(jax.random.fold_in(splits[14], 71), 0)
    norm_gain = jnp.clip(1.0 + 0.1 * jax.random.normal(splits[7], (D,), jnp.float32), 0.5, 1.5).astype(jnp.bfloat16)
    out_proj = bell_draw(splits[8], (H * HD, D), (H * HD) ** -0.5, 0.125, ((0, 2),))
    router = bell_draw(splits[9], (D, EXPERTS), D ** -0.5, 0.125)
    routes_keys = jax.random.split(jax.random.fold_in(splits[10], 1), REQS * DRAFT // (RK * DRAFT))
    routes_turns = jax.random.permutation(jax.random.fold_in(splits[10], 3), REQS * DRAFT // (RK * DRAFT))
    routes = jax.vmap(lambda own, number: routed_block(jax.random.fold_in(splits[10], 2), own, number, RK * DRAFT, EXPERTS, TOPK, CAP, 2))(routes_keys, routes_turns).reshape((REQS, DRAFT, TOPK))
    gate_w = bell_draw(splits[11], (EXPERTS, D, FF), D ** -0.5, 0.125, ((0, 16), (2, 2)))
    up_w = bell_draw(splits[12], (EXPERTS, D, FF), D ** -0.5, 0.125, ((0, 16), (2, 2)))
    down_w = bell_draw(splits[13], (EXPERTS, FF, D), FF ** -0.5, 0.1875, ((0, 16), (1, 2)))
    return {"queries": queries, "draft_kv": draft_kv, "kv_pool": kv_pool, "page_table": page_table, "cache_lens": cache_lens, "parents": parents, "hidden": hidden, "norm_gain": norm_gain, "out_proj": out_proj, "router": router, "routes": routes, "gate_w": gate_w, "up_w": up_w, "down_w": down_w}


NEG_FILL = -1e+30
EPS_NORM = 1e-06

def ancestry(parents):
    positions = jnp.arange(DRAFT, dtype=jnp.int32)
    linked = (parents[:, :, None] == positions[None, None, :]).astype(jnp.float32)
    linked = linked + jnp.eye(DRAFT, dtype=jnp.float32)[None]
    for doubling in range((DRAFT - 1).bit_length()):
        linked = jnp.minimum(jnp.einsum('nij,njk->nik', linked, linked, precision=lax.Precision.HIGHEST), 1.0)
    return linked

def slot_numbers(flat_routes):
    expert_ids = jnp.arange(EXPERTS, dtype=jnp.int32)
    picked = (flat_routes[:, None] == expert_ids[None, :]).astype(jnp.int32)
    earlier = jnp.cumsum(picked, axis=0) - picked
    return flat_routes * CAP + lax.optimization_barrier(jnp.sum(earlier * picked, axis=1))

def set_partials(query_rows, cache_keys, cache_values, draft_keys, draft_values, cache_seen, draft_seen):
    key_rows = jnp.concatenate([cache_keys, draft_keys], axis=0).astype(jnp.float32).reshape(-1, H, HD)
    value_rows = jnp.concatenate([cache_values, draft_values], axis=0).astype(jnp.float32).reshape(-1, H, HD)
    query_heads = query_rows.astype(jnp.float32).reshape(DRAFT, H, HD)
    visible = jnp.concatenate([jnp.broadcast_to(cache_seen[None, :], (DRAFT, cache_seen.shape[0])), draft_seen], axis=1)
    scores = jnp.einsum('qhd,khd->hqk', query_heads, key_rows, precision=lax.Precision.HIGHEST) * HD ** (-0.5)
    scores = jnp.where(visible[None], scores, NEG_FILL)
    row_max = lax.optimization_barrier(jnp.max(scores, axis=2))
    weights = jnp.where(visible[None], jnp.exp(scores - row_max[:, :, None]), 0.0)
    row_sum = lax.optimization_barrier(jnp.sum(weights, axis=2))
    rounded = lax.optimization_barrier(weights.astype(jnp.bfloat16)).astype(jnp.float32)
    weighted = jnp.einsum('hqk,khd->qhd', rounded, value_rows, precision=lax.Precision.HIGHEST)
    return (jnp.transpose(row_max), jnp.transpose(row_sum), weighted)

def reference(queries, draft_kv, kv_pool, page_table, cache_lens, parents, hidden, norm_gain, out_proj, router, routes, gate_w, up_w, down_w):
    draft_share = DRAFT // SETS

    def attend(request_item):
        query_rows, draft_keys, draft_values, table_rows, length, parent, block_index = request_item
        pool_index = ((block_index * SETS + jnp.arange(SETS, dtype=jnp.int32)) * (RK * PPD))[None, :] + table_rows
        page_keys = jnp.transpose(kv_pool[0][pool_index], (1, 0, 2, 3)).reshape(SETS, PPD * PAGE, H * HD)
        page_values = jnp.transpose(kv_pool[1][pool_index], (1, 0, 2, 3)).reshape(SETS, PPD * PAGE, H * HD)
        page_ids = jnp.arange(PPD, dtype=jnp.int32)[None, :, None] * SETS + jnp.arange(SETS, dtype=jnp.int32)[:, None, None]
        positions = (page_ids * PAGE + jnp.arange(PAGE, dtype=jnp.int32)[None, None, :]).reshape(SETS, PPD * PAGE)
        cache_seen = positions < length
        linked = ancestry(parent[None])[0]
        draft_seen = jnp.transpose(linked.reshape(DRAFT, SETS, draft_share), (1, 0, 2)) > 0.5
        set_max, set_sum, set_acc = jax.vmap(set_partials, in_axes=(None, 0, 0, 0, 0, 0, 0))(query_rows, page_keys, page_values, draft_keys.reshape(SETS, draft_share, H * HD), draft_values.reshape(SETS, draft_share, H * HD), cache_seen, draft_seen)
        overall_max = lax.optimization_barrier(jnp.max(set_max, axis=0))
        set_scale = jnp.exp(set_max - overall_max[None])
        row_sum = lax.optimization_barrier(jnp.sum(set_scale * set_sum, axis=0))
        weighted = lax.optimization_barrier(jnp.sum(set_scale[..., None] * set_acc, axis=0))
        return (weighted / row_sum[..., None]).astype(jnp.bfloat16).reshape(DRAFT, H * HD)
    block_of = jnp.arange(REQS, dtype=jnp.int32) // RK
    attended = lax.map(attend, (queries, draft_kv[0], draft_kv[1], page_table, cache_lens, parents, block_of))
    token_count = REQS * DRAFT
    projected = jnp.dot(attended.reshape(token_count, H * HD), out_proj, preferred_element_type=jnp.float32)
    residual = hidden.reshape(token_count, D).astype(jnp.float32) + projected
    mean_sq = lax.optimization_barrier(jnp.mean(residual * residual, axis=1, keepdims=True))
    normed = (residual * lax.rsqrt(mean_sq + EPS_NORM) * norm_gain.astype(jnp.float32)[None, :]).astype(jnp.bfloat16)
    logits = jnp.dot(normed, router, preferred_element_type=jnp.float32)
    chosen = routes.reshape(token_count, TOPK)
    gate_values = jax.nn.sigmoid(jnp.take_along_axis(logits, chosen, axis=1))
    block_rows = RK * DRAFT
    block_count = REQS // RK
    slot_of = jax.vmap(slot_numbers)(chosen.reshape(block_count, block_rows * TOPK))
    owner_rows = jnp.arange(block_count, dtype=jnp.int32)[:, None] * block_rows + jnp.arange(block_rows * TOPK, dtype=jnp.int32)[None, :] // TOPK
    block_ids = jnp.broadcast_to(jnp.arange(block_count, dtype=jnp.int32)[:, None], slot_of.shape)
    token_table = jnp.full((block_count, EXPERTS * CAP), -1, jnp.int32).at[block_ids, slot_of].set(owner_rows)
    gate_table = jnp.zeros((block_count, EXPERTS * CAP), jnp.float32).at[block_ids, slot_of].set(gate_values.reshape(block_count, block_rows * TOPK))
    token_table = jnp.transpose(token_table.reshape(block_count, EXPERTS, CAP), (1, 0, 2)).reshape(EXPERTS, block_count * CAP)
    gate_table = jnp.transpose(gate_table.reshape(block_count, EXPERTS, CAP), (1, 0, 2)).reshape(EXPERTS, block_count * CAP)
    slice_width = FF // SETS

    def expert_step(moe_total, expert_item):
        gate_mat, up_mat, down_mat, token_ids, gate_vals = expert_item
        present = token_ids >= 0
        safe_ids = jnp.maximum(token_ids, 0)
        rows_in = normed[safe_ids]
        gate_pre = jnp.dot(rows_in, gate_mat, preferred_element_type=jnp.float32)
        up_pre = jnp.dot(rows_in, up_mat, preferred_element_type=jnp.float32)
        activity = (jax.nn.silu(gate_pre) * up_pre).astype(jnp.bfloat16)
        contrib = jnp.zeros((rows_in.shape[0], D), jnp.float32)
        for slice_index in range(SETS):
            slice_part = jnp.dot(activity[:, slice_index * slice_width:(slice_index + 1) * slice_width], down_mat[slice_index * slice_width:(slice_index + 1) * slice_width], preferred_element_type=jnp.float32)
            slice_part = lax.optimization_barrier(slice_part.astype(jnp.bfloat16)).astype(jnp.float32)
            contrib = contrib + gate_vals[:, None] * slice_part
        contrib = jnp.where(present[:, None], contrib, 0.0)
        return (moe_total.at[safe_ids].add(contrib), None)
    moe_total, unused = lax.scan(expert_step, jnp.zeros((token_count, D), jnp.float32), (gate_w, up_w, down_w, token_table, gate_table))
    return (residual + moe_total).astype(jnp.bfloat16).reshape(REQS, DRAFT, D)
```

```python
import jax
import jax.numpy as jnp
from jax import lax
from jax.sharding import PartitionSpec as P

D = 2048
H = 16
EXPERTS = 64
TOPK = 8
CAP = 16


NEG_FILL = -1e30
EPS_NORM = 1e-06


def merged(x, axis, combine):
    everything = jax.tree.map(
        lambda part, kind: lax.all_gather(part.astype(kind), axis),
        x,
        (jnp.bfloat16, jnp.bfloat16, jnp.bfloat16),
    )

    def take(k):
        return jax.tree.map(lambda part, own: part[k].astype(own.dtype), everything, x)

    return lax.fori_loop(
        1, lax.axis_size(axis), lambda k, so_far: combine(so_far, take(k)), take(0)
    )


def ancestry(parents, draft_len):
    positions = jnp.arange(draft_len, dtype=jnp.int32)
    linked = (parents[:, :, None] == positions[None, None, :]).astype(jnp.float32)
    linked = linked + jnp.eye(draft_len, dtype=jnp.float32)[None]
    for doubling in range((draft_len - 1).bit_length()):
        linked = jnp.minimum(
            jnp.einsum("nij,njk->nik", linked, linked, precision=lax.Precision.HIGHEST), 1.0
        )
    return linked


def merge_pair(former, latter):
    new_max = jnp.maximum(former[0], latter[0])
    former_scale = jnp.exp(former[0] - new_max)
    latter_scale = jnp.exp(latter[0] - new_max)
    return (
        new_max,
        former[1] * former_scale + latter[1] * latter_scale,
        former[2] * former_scale[..., None] + latter[2] * latter_scale[..., None],
    )


def local(
    queries,
    draft_kv,
    kv_pool,
    page_table,
    cache_lens,
    parents,
    hidden,
    norm_gain,
    out_proj,
    router,
    routes,
    gate_w,
    up_w,
    down_w,
):
    set_count = lax.axis_size("exp")
    my_set = lax.axis_index("exp")
    req_count, draft_len, feature_width = queries.shape
    head_dim = feature_width // H
    head_share = H // set_count
    page_count = page_table.shape[1]
    page_len = kv_pool.shape[2]
    draft_share = draft_kv.shape[2]
    slot_ids = jnp.arange(page_count, dtype=jnp.int32)
    page_of = jnp.sum(
        jnp.where(page_table[:, :, 0][:, :, None] == slot_ids, slot_ids[None, :, None], 0), axis=1
    )
    cache_keys = kv_pool[0].reshape(req_count, page_count * page_len, feature_width)
    cache_values = kv_pool[1].reshape(req_count, page_count * page_len, feature_width)
    positions = (
        (page_of * set_count + my_set)[:, :, None] * page_len
        + jnp.arange(page_len, dtype=jnp.int32)[None, None, :]
    ).reshape(req_count, -1)
    cache_seen = positions < cache_lens[:, None]
    linked = ancestry(parents, draft_len)
    draft_seen = lax.dynamic_slice_in_dim(linked, my_set * draft_share, draft_share, 2) > 0.5
    visible = jnp.concatenate(
        [
            jnp.broadcast_to(cache_seen[:, None, :], (req_count, draft_len, page_count * page_len)),
            draft_seen,
        ],
        axis=2,
    )
    key_rows = jnp.concatenate([cache_keys, draft_kv[0]], axis=1).reshape(
        req_count, -1, H, head_dim
    )
    value_rows = jnp.concatenate([cache_values, draft_kv[1]], axis=1).reshape(
        req_count, -1, H, head_dim
    )
    query_rows = queries.reshape(req_count, draft_len, H, head_dim)
    scores = jnp.einsum(
        "rqhd,rkhd->rhqk", query_rows, key_rows, preferred_element_type=jnp.float32
    ) * head_dim ** (-0.5)
    scores = jnp.where(visible[:, None], scores, NEG_FILL)
    row_max = jnp.max(scores, axis=3)
    weights = jnp.where(visible[:, None], jnp.exp(scores - row_max[..., None]), 0.0)
    row_sum = jnp.sum(weights, axis=3)
    weighted = jnp.einsum(
        "rhqk,rkhd->rqhd",
        weights.astype(jnp.bfloat16),
        value_rows,
        preferred_element_type=jnp.float32,
    )
    row_max = jnp.transpose(row_max, (0, 2, 1))
    row_sum = jnp.transpose(row_sum, (0, 2, 1))
    row_max, row_sum, weighted = merged((row_max, row_sum, weighted), "exp", merge_pair)
    attended = (weighted / row_sum[..., None]).astype(jnp.bfloat16)
    attended = lax.dynamic_slice_in_dim(attended, my_set * head_share, head_share, 2)
    token_rows = req_count * draft_len
    attended = attended.reshape(token_rows, head_share * head_dim)
    partial_value = jnp.dot(attended, out_proj, preferred_element_type=jnp.float32)
    projected = lax.psum(partial_value.astype(jnp.bfloat16), "exp").astype(jnp.float32)
    residual = hidden.reshape(token_rows, D).astype(jnp.float32) + projected
    mean_sq = jnp.mean(residual * residual, axis=1, keepdims=True)
    normed = (
        residual * lax.rsqrt(mean_sq + EPS_NORM) * norm_gain.astype(jnp.float32)[None, :]
    ).astype(jnp.bfloat16)
    spread = ("kv", "seq")
    local_experts = gate_w.shape[0]
    column_count = D // set_count
    my_block = lax.axis_index("kv") * lax.axis_size("seq") + lax.axis_index("seq")
    all_routes = lax.all_gather(routes.reshape(token_rows, TOPK), spread)
    sources = all_routes.shape[0]
    expert_ids = my_block * local_experts + jnp.arange(local_experts, dtype=jnp.int32)
    member = jnp.any(all_routes[:, None] == expert_ids[None, :, None, None], axis=3).astype(jnp.int32)
    rank = jnp.cumsum(member, axis=2) - member
    chosen = (member[:, :, None, :] > 0) & (
        rank[:, :, None, :] == jnp.arange(CAP, dtype=jnp.int32)[None, None, :, None]
    )
    chosen = chosen.astype(jnp.bfloat16)
    all_rows = lax.all_gather(normed, spread)
    picked = jnp.einsum("sect,std->escd", chosen, all_rows, preferred_element_type=jnp.float32)
    picked = picked.astype(jnp.bfloat16).reshape(local_experts, sources * CAP, D)
    own_router = lax.dynamic_slice_in_dim(router, my_block * local_experts, local_experts, 1)
    logits = jnp.einsum("erd,de->er", picked, own_router, preferred_element_type=jnp.float32)
    gate_pre = jnp.einsum("erd,edf->erf", picked, gate_w, preferred_element_type=jnp.float32)
    up_pre = jnp.einsum("erd,edf->erf", picked, up_w, preferred_element_type=jnp.float32)
    activity = jax.nn.silu(gate_pre) * up_pre * jax.nn.sigmoid(logits)[:, :, None]
    finished = jnp.einsum(
        "erf,efd->erd", activity.astype(jnp.bfloat16), down_w, preferred_element_type=jnp.float32
    ).astype(jnp.bfloat16).reshape(local_experts, sources, CAP, D)
    combined = jnp.einsum("sect,escd->std", chosen, finished, preferred_element_type=jnp.float32)
    combined = combined.astype(jnp.bfloat16).reshape(sources, token_rows, set_count, column_count)
    combined = jnp.transpose(combined, (0, 2, 1, 3)).reshape(-1, token_rows, column_count)
    summed_share = lax.psum_scatter(
        combined, ("kv", "seq", "exp"), scatter_dimension=0, tiled=True
    )[0].astype(jnp.float32)
    own_columns = lax.dynamic_slice_in_dim(residual, my_set * column_count, column_count, 1)
    return (
        (own_columns + summed_share)
        .astype(jnp.bfloat16)
        .reshape(req_count, draft_len, column_count)
    )


def solution(mesh):
    in_specs = (
        P(("kv", "seq"), None, None),
        P(None, ("kv", "seq"), "exp", None),
        P(None, ("kv", "seq", "exp"), None, None),
        P(("kv", "seq"), None, "exp"),
        P(("kv", "seq")),
        P(("kv", "seq"), None),
        P(("kv", "seq"), None, None),
        P(),
        P("exp", None),
        P(),
        P(("kv", "seq"), None, None),
        P(("kv", "seq"), None, "exp"),
        P(("kv", "seq"), None, "exp"),
        P(("kv", "seq"), "exp", None),
    )
    out_specs = P(("kv", "seq"), None, "exp")
    return jax.shard_map(local, mesh=mesh, in_specs=in_specs, out_specs=out_specs, check_vma=False)
```

```python
import functools

import jax
import jax.numpy as jnp
from jax import lax
from jax.experimental import pallas as pl
from jax.experimental.pallas import tpu as pltpu
from jax.sharding import PartitionSpec as P

D = 2048
H = 16
EXPERTS = 64
TOPK = 8
CAP = 16


NEG_FILL = -1e30
EPS_NORM = 1e-06


MESH = pl.DeviceIdType.MESH


def bits_of(axis):
    return [(axis, bit) for bit in range((lax.axis_size(axis) - 1).bit_length())]


def my_bit(stage):
    axis, bit = stage
    return (lax.axis_index(axis) // 2**bit) % 2


def partner(stage):
    axis, bit = stage
    return {axis: lax.axis_index(axis) + (1 - 2 * my_bit(stage)) * 2**bit}


def greet(stages):
    barrier = pltpu.get_barrier_semaphore()
    for stage in stages:
        pl.semaphore_signal(barrier, inc=1, device_id=partner(stage), device_id_type=MESH)
    pl.semaphore_wait(barrier, len(stages))


def gather_kernel(orders, *refs):
    count = len(orders)
    ins, outs = refs[:count], refs[count : 2 * count]
    send_sem, recv_sem = refs[2 * count :]
    for i, order in enumerate(orders):
        place = sum(my_bit(stage) * 2**k for k, stage in enumerate(order))
        outs[i][place] = ins[i][...]
    greet(sorted(orders[0]))
    copies = [[] for order in orders]
    for k in range(len(orders[0])):
        for i, order in enumerate(orders):
            if k > 0:
                copies[i][k - 1].wait_recv()
            base = sum(my_bit(stage) * 2**j for j, stage in enumerate(order) if j >= k)
            region = outs[i].at[pl.ds(base, 2**k)]
            copy = pltpu.make_async_remote_copy(
                src_ref=region,
                dst_ref=region,
                send_sem=send_sem.at[i, k],
                recv_sem=recv_sem.at[i, k],
                device_id=partner(order[k]),
                device_id_type=MESH,
            )
            copy.start()
            copies[i].append(copy)
    for i in range(count):
        copies[i][-1].wait_recv()
    for i in range(count):
        for copy in copies[i]:
            copy.wait_send()


def gather_all(parts, orders, ident):
    steps = len(orders[0])
    vmem = pl.BlockSpec(memory_space=pltpu.VMEM)
    return pl.pallas_call(
        functools.partial(gather_kernel, orders),
        out_shape=[jax.ShapeDtypeStruct((2**steps,) + part.shape, part.dtype) for part in parts],
        in_specs=[vmem] * len(parts),
        out_specs=[vmem] * len(parts),
        scratch_shapes=[
            pltpu.SemaphoreType.DMA((len(parts), steps)),
            pltpu.SemaphoreType.DMA((len(parts), steps)),
        ],
        compiler_params=pltpu.CompilerParams(
            collective_id=ident, has_side_effects=True, vmem_limit_bytes=56 * 2**20
        ),
    )(*parts)


def reduce_kernel(orders, *refs):
    count, steps = len(orders), len(orders[0])
    ins, outs = refs[:count], refs[count : 2 * count]
    buffers = refs[2 * count : 2 * count + count * steps]
    send_sem, recv_sem = refs[2 * count + count * steps :]
    greet(sorted(orders[0]))
    copies = [[] for order in orders]

    def held(i, k):
        return ins[i] if k == 0 else buffers[i * steps + k - 1]

    def add_in(i, k):
        half = 2 ** (steps - 1 - k)
        base = my_bit(orders[i][k]) * half
        mine, came = held(i, k), buffers[i * steps + k]

        def one(j, carry):
            total = mine[base + j].astype(jnp.float32) + came[j].astype(jnp.float32)
            if k == steps - 1:
                outs[i][...] = total
            else:
                came[j] = total.astype(came.dtype)
            return carry

        lax.fori_loop(0, half, one, 0)

    for k in range(steps):
        half = 2 ** (steps - 1 - k)
        for i, order in enumerate(orders):
            if k > 0:
                copies[i][k - 1].wait_recv()
                add_in(i, k - 1)
            copy = pltpu.make_async_remote_copy(
                src_ref=held(i, k).at[pl.ds((1 - my_bit(order[k])) * half, half)],
                dst_ref=buffers[i * steps + k],
                send_sem=send_sem.at[i, k],
                recv_sem=recv_sem.at[i, k],
                device_id=partner(order[k]),
                device_id_type=MESH,
            )
            copy.start()
            copies[i].append(copy)
    for i in range(count):
        copies[i][-1].wait_recv()
        add_in(i, steps - 1)
    for i in range(count):
        for copy in copies[i]:
            copy.wait_send()


def reduce_all(parts, orders, ident):
    steps = len(orders[0])
    vmem = pl.BlockSpec(memory_space=pltpu.VMEM)
    return pl.pallas_call(
        functools.partial(reduce_kernel, orders),
        out_shape=[jax.ShapeDtypeStruct(part.shape[1:], jnp.float32) for part in parts],
        in_specs=[vmem] * len(parts),
        out_specs=[vmem] * len(parts),
        scratch_shapes=[
            pltpu.VMEM((2 ** (steps - 1 - k),) + part.shape[1:], part.dtype)
            for part in parts
            for k in range(steps)
        ]
        + [
            pltpu.SemaphoreType.DMA((len(parts), steps)),
            pltpu.SemaphoreType.DMA((len(parts), steps)),
        ],
        compiler_params=pltpu.CompilerParams(
            collective_id=ident, has_side_effects=True, vmem_limit_bytes=56 * 2**20
        ),
    )(*parts)


def bit_axes():
    return [stage for axis in ("kv", "seq", "exp") for stage in bits_of(axis)[::-1]]


def spread_bits(x, order):
    names = bit_axes()
    x = x.reshape((2,) * len(names) + x.shape[1:])
    tail = range(len(names), x.ndim)
    x = jnp.transpose(x, [names.index(stage) for stage in order] + list(tail))
    return x.reshape((2 ** len(names),) + x.shape[len(names) :])


def collect_bits(x, order):
    names = bit_axes()
    x = x.reshape((2,) * len(names) + x.shape[1:])
    tail = range(len(names), x.ndim)
    x = jnp.transpose(x, [order.index(stage) for stage in names] + list(tail))
    return x.reshape((2 ** len(names),) + x.shape[len(names) :])


def stream_orders(count):
    kv, seq, exp = bits_of("kv"), bits_of("seq"), bits_of("exp")
    orders = (kv + exp + seq[::-1], kv[:1] + exp + kv[1:] + seq[::-1])
    return [orders[i % 2] for i in range(count)]


def columns_cut(x, width):
    return [x[..., k : k + width] for k in range(0, x.shape[-1], width)]


def ancestry(parents, draft_len):
    positions = jnp.arange(draft_len, dtype=jnp.int32)
    linked = (parents[:, :, None] == positions[None, None, :]).astype(jnp.float32)
    linked = linked + jnp.eye(draft_len, dtype=jnp.float32)[None]
    for doubling in range((draft_len - 1).bit_length()):
        linked = jnp.minimum(
            jnp.einsum("nij,njk->nik", linked, linked, precision=lax.Precision.HIGHEST), 1.0
        )
    return linked


def merge_pair(former, latter):
    new_max = jnp.maximum(former[0], latter[0])
    former_scale = jnp.exp(former[0] - new_max)
    latter_scale = jnp.exp(latter[0] - new_max)
    return (
        new_max,
        former[1] * former_scale + latter[1] * latter_scale,
        former[2] * former_scale[..., None] + latter[2] * latter_scale[..., None],
    )


def local(
    queries,
    draft_kv,
    kv_pool,
    page_table,
    cache_lens,
    parents,
    hidden,
    norm_gain,
    out_proj,
    router,
    routes,
    gate_w,
    up_w,
    down_w,
):
    set_count = lax.axis_size("exp")
    my_set = lax.axis_index("exp")
    req_count, draft_len, feature_width = queries.shape
    head_dim = feature_width // H
    head_share = H // set_count
    page_count = page_table.shape[1]
    page_len = kv_pool.shape[2]
    draft_share = draft_kv.shape[2]
    slot_ids = jnp.arange(page_count, dtype=jnp.int32)
    page_of = jnp.sum(
        jnp.where(page_table[:, :, 0][:, :, None] == slot_ids, slot_ids[None, :, None], 0), axis=1
    )
    cache_keys = kv_pool[0].reshape(req_count, page_count * page_len, feature_width)
    cache_values = kv_pool[1].reshape(req_count, page_count * page_len, feature_width)
    positions = (
        (page_of * set_count + my_set)[:, :, None] * page_len
        + jnp.arange(page_len, dtype=jnp.int32)[None, None, :]
    ).reshape(req_count, -1)
    cache_seen = positions < cache_lens[:, None]
    linked = ancestry(parents, draft_len)
    draft_seen = lax.dynamic_slice_in_dim(linked, my_set * draft_share, draft_share, 2) > 0.5
    visible = jnp.concatenate(
        [
            jnp.broadcast_to(cache_seen[:, None, :], (req_count, draft_len, page_count * page_len)),
            draft_seen,
        ],
        axis=2,
    )
    key_rows = jnp.concatenate([cache_keys, draft_kv[0]], axis=1).reshape(
        req_count, -1, H, head_dim
    )
    value_rows = jnp.concatenate([cache_values, draft_kv[1]], axis=1).reshape(
        req_count, -1, H, head_dim
    )
    query_rows = queries.reshape(req_count, draft_len, H, head_dim)
    scores = jnp.einsum(
        "rqhd,rkhd->rhqk", query_rows, key_rows, preferred_element_type=jnp.float32
    ) * head_dim ** (-0.5)
    scores = jnp.where(visible[:, None], scores, NEG_FILL)
    row_max = jnp.max(scores, axis=3)
    weights = jnp.where(visible[:, None], jnp.exp(scores - row_max[..., None]), 0.0)
    row_sum = jnp.sum(weights, axis=3)
    weighted = jnp.einsum(
        "rhqk,rkhd->rqhd",
        weights.astype(jnp.bfloat16),
        value_rows,
        preferred_element_type=jnp.float32,
    )
    row_max = jnp.transpose(row_max, (0, 2, 1))
    row_sum = jnp.transpose(row_sum, (0, 2, 1))
    token_rows = req_count * draft_len
    column_count = D // set_count
    exp_bits = bits_of("exp")
    stats = jnp.concatenate([row_max, row_sum], axis=2).reshape(token_rows, 2 * H)
    stats = jnp.pad(stats, ((0, 0), (0, 128 - 2 * H)))
    all_weighted, all_stats = gather_all(
        [weighted.astype(jnp.bfloat16).reshape(token_rows, D), stats], [exp_bits, exp_bits], 1
    )

    def one_set(k):
        return (
            all_stats[k, :, :H].reshape(row_max.shape),
            all_stats[k, :, H : 2 * H].reshape(row_sum.shape),
            all_weighted[k].astype(jnp.float32).reshape(weighted.shape),
        )

    row_max, row_sum, weighted = functools.reduce(
        merge_pair, [one_set(k) for k in range(set_count)]
    )
    attended = (weighted / row_sum[..., None]).astype(jnp.bfloat16)
    attended = lax.dynamic_slice_in_dim(attended, my_set * head_share, head_share, 2)
    attended = attended.reshape(token_rows, head_share * head_dim)
    partial_value = jnp.dot(attended, out_proj, preferred_element_type=jnp.float32)
    by_columns = jnp.transpose(
        partial_value.astype(jnp.bfloat16).reshape(token_rows, set_count, column_count), (1, 0, 2)
    )
    (projected,) = reduce_all([by_columns], [exp_bits[::-1]], 2)

    def own_part(x):
        return lax.dynamic_slice_in_dim(x, my_set * column_count, column_count, x.ndim - 1)

    residual = own_part(hidden.reshape(token_rows, D)).astype(jnp.float32) + projected
    own_sq = jnp.sum(residual * residual, axis=1, keepdims=True)
    (all_sq,) = gather_all([jnp.broadcast_to(own_sq, (token_rows, 128))], [exp_bits], 3)
    mean_sq = jnp.sum(all_sq[:, :, :1], axis=0) / D
    normed = (
        residual * lax.rsqrt(mean_sq + EPS_NORM) * own_part(norm_gain).astype(jnp.float32)[None, :]
    ).astype(jnp.bfloat16)
    width = max(128, column_count // 4)
    streams = column_count // width
    orders = stream_orders(streams)
    local_experts = gate_w.shape[0]
    my_block = lax.axis_index("kv") * lax.axis_size("seq") + lax.axis_index("seq")
    routes_row = jnp.pad(
        jnp.transpose(routes.reshape(token_rows, TOPK)), ((0, 0), (0, -token_rows % 128))
    )
    gathered = gather_all(
        columns_cut(normed, width) + [routes_row],
        [order[::-1] for order in orders] + [orders[0][::-1]],
        4,
    )
    sources = lax.axis_size("kv") * lax.axis_size("seq")
    all_routes = collect_bits(gathered[-1], orders[0]).reshape(
        (sources, set_count) + routes_row.shape
    )[:, 0, :, :token_rows]
    all_routes = jnp.transpose(all_routes, (0, 2, 1))
    by_stream = [
        collect_bits(part, order).reshape(sources, set_count, token_rows, width)
        for part, order in zip(gathered, orders)
    ]
    all_rows = jnp.transpose(jnp.stack(by_stream, axis=3), (0, 2, 1, 3, 4)).reshape(
        sources, token_rows, D
    )
    expert_ids = my_block * local_experts + jnp.arange(local_experts, dtype=jnp.int32)
    member = jnp.any(all_routes[:, None] == expert_ids[None, :, None, None], axis=3).astype(jnp.int32)
    rank = jnp.cumsum(member, axis=2) - member
    chosen = (member[:, :, None, :] > 0) & (
        rank[:, :, None, :] == jnp.arange(CAP, dtype=jnp.int32)[None, None, :, None]
    )
    chosen = chosen.astype(jnp.bfloat16)
    picked = jnp.einsum("sect,std->escd", chosen, all_rows, preferred_element_type=jnp.float32)
    picked = picked.astype(jnp.bfloat16).reshape(local_experts, sources * CAP, D)
    own_router = lax.dynamic_slice_in_dim(router, my_block * local_experts, local_experts, 1)
    logits = jnp.einsum("erd,de->er", picked, own_router, preferred_element_type=jnp.float32)
    gate_pre = jnp.einsum("erd,edf->erf", picked, gate_w, preferred_element_type=jnp.float32)
    up_pre = jnp.einsum("erd,edf->erf", picked, up_w, preferred_element_type=jnp.float32)
    activity = jax.nn.silu(gate_pre) * up_pre * jax.nn.sigmoid(logits)[:, :, None]
    finished = jnp.einsum(
        "erf,efd->erd", activity.astype(jnp.bfloat16), down_w, preferred_element_type=jnp.float32
    ).astype(jnp.bfloat16).reshape(local_experts, sources, CAP, D)
    combined = jnp.einsum("sect,escd->std", chosen, finished, preferred_element_type=jnp.float32)
    combined = combined.astype(jnp.bfloat16).reshape(sources, token_rows, set_count, column_count)
    combined = jnp.transpose(combined, (0, 2, 1, 3)).reshape(-1, token_rows, column_count)
    summed_share = jnp.concatenate(
        reduce_all(
            [spread_bits(part, order) for part, order in zip(columns_cut(combined, width), orders)],
            orders,
            5,
        ),
        axis=1,
    )
    return (
        (residual + summed_share)
        .astype(jnp.bfloat16)
        .reshape(req_count, draft_len, column_count)
    )


def solution(mesh):
    in_specs = (
        P(("kv", "seq"), None, None),
        P(None, ("kv", "seq"), "exp", None),
        P(None, ("kv", "seq", "exp"), None, None),
        P(("kv", "seq"), None, "exp"),
        P(("kv", "seq")),
        P(("kv", "seq"), None),
        P(("kv", "seq"), None, None),
        P(),
        P("exp", None),
        P(),
        P(("kv", "seq"), None, None),
        P(("kv", "seq"), None, "exp"),
        P(("kv", "seq"), None, "exp"),
        P(("kv", "seq"), "exp", None),
    )
    out_specs = P(("kv", "seq"), None, "exp")
    return jax.shard_map(local, mesh=mesh, in_specs=in_specs, out_specs=out_specs, check_vma=False)
```

```python
import functools

import jax
import jax.numpy as jnp
from jax import lax
from jax.experimental import pallas as pl
from jax.experimental.pallas import tpu as pltpu
from jax.sharding import PartitionSpec as P

D = 2048
H = 16
EXPERTS = 64
TOPK = 8
CAP = 16


NEG_FILL = -1e30
EPS_NORM = 1e-06


MESH = pl.DeviceIdType.MESH


def bits_of(axis):
    return [(axis, bit) for bit in range((lax.axis_size(axis) - 1).bit_length())]


def my_bit(stage):
    axis, bit = stage
    return (lax.axis_index(axis) // 2**bit) % 2


def partner(stage):
    axis, bit = stage
    return {axis: lax.axis_index(axis) + (1 - 2 * my_bit(stage)) * 2**bit}


def starts_of(parts, steps):
    if steps < 3:
        return [0] * len(parts)
    return [2 if i // 2 % 2 == 1 else 0 for i in range(len(parts))]


def greet(stages):
    barrier = pltpu.get_barrier_semaphore()
    for stage in stages:
        pl.semaphore_signal(barrier, inc=1, device_id=partner(stage), device_id_type=MESH)
    pl.semaphore_wait(barrier, len(stages))


def gather_kernel(orders, starts, *refs):
    count = len(orders)
    ins, outs = refs[:count], refs[count : 2 * count]
    send_sem, recv_sem = refs[2 * count :]
    for i, order in enumerate(orders):
        place = sum(my_bit(stage) * 2**k for k, stage in enumerate(order))
        outs[i][place] = ins[i][...]
    greet(sorted(orders[0]))
    copies = [[] for order in orders]
    for slot in range(len(orders[0]) + max(starts)):
        for i, order in enumerate(orders):
            k = slot - starts[i]
            if k < 0 or k > len(order):
                continue
            if k > 0:
                copies[i][k - 1].wait_recv()
            if k == len(order):
                continue
            base = sum(my_bit(stage) * 2**j for j, stage in enumerate(order) if j >= k)
            region = outs[i].at[pl.ds(base, 2**k)]
            copy = pltpu.make_async_remote_copy(
                src_ref=region,
                dst_ref=region,
                send_sem=send_sem.at[i, k],
                recv_sem=recv_sem.at[i, k],
                device_id=partner(order[k]),
                device_id_type=MESH,
            )
            copy.start()
            copies[i].append(copy)
    for i, order in enumerate(orders):
        if starts[i] == max(starts):
            copies[i][-1].wait_recv()
    for i in range(count):
        for copy in copies[i]:
            copy.wait_send()


def gather_all(parts, orders, ident):
    steps = len(orders[0])
    vmem = pl.BlockSpec(memory_space=pltpu.VMEM)
    return pl.pallas_call(
        functools.partial(gather_kernel, orders, starts_of(parts, steps)),
        out_shape=[jax.ShapeDtypeStruct((2**steps,) + part.shape, part.dtype) for part in parts],
        in_specs=[vmem] * len(parts),
        out_specs=[vmem] * len(parts),
        scratch_shapes=[
            pltpu.SemaphoreType.DMA((len(parts), steps)),
            pltpu.SemaphoreType.DMA((len(parts), steps)),
        ],
        compiler_params=pltpu.CompilerParams(
            collective_id=ident, has_side_effects=True, vmem_limit_bytes=56 * 2**20
        ),
    )(*parts)


def reduce_kernel(orders, starts, *refs):
    count, steps = len(orders), len(orders[0])
    ins, outs = refs[:count], refs[count : 2 * count]
    buffers = refs[2 * count : 2 * count + count * steps]
    send_sem, recv_sem = refs[2 * count + count * steps :]
    greet(sorted(orders[0]))
    copies = [[] for order in orders]

    def held(i, k):
        return ins[i] if k == 0 else buffers[i * steps + k - 1]

    def add_in(i, k):
        half = 2 ** (steps - 1 - k)
        base = my_bit(orders[i][k]) * half
        mine, came = held(i, k), buffers[i * steps + k]

        def one(j, carry):
            total = mine[base + j].astype(jnp.float32) + came[j].astype(jnp.float32)
            if k == steps - 1:
                outs[i][...] = total
            else:
                came[j] = total.astype(came.dtype)
            return carry

        lax.fori_loop(0, half, one, 0)

    for slot in range(steps + max(starts)):
        for i, order in enumerate(orders):
            k = slot - starts[i]
            if k < 0 or k > steps:
                continue
            if k > 0:
                copies[i][k - 1].wait_recv()
                add_in(i, k - 1)
            if k == steps:
                continue
            half = 2 ** (steps - 1 - k)
            copy = pltpu.make_async_remote_copy(
                src_ref=held(i, k).at[pl.ds((1 - my_bit(order[k])) * half, half)],
                dst_ref=buffers[i * steps + k],
                send_sem=send_sem.at[i, k],
                recv_sem=recv_sem.at[i, k],
                device_id=partner(order[k]),
                device_id_type=MESH,
            )
            copy.start()
            copies[i].append(copy)
    for i in range(count):
        if starts[i] == max(starts):
            copies[i][-1].wait_recv()
            add_in(i, steps - 1)
    for i in range(count):
        for copy in copies[i]:
            copy.wait_send()


def reduce_all(parts, orders, ident):
    steps = len(orders[0])
    vmem = pl.BlockSpec(memory_space=pltpu.VMEM)
    return pl.pallas_call(
        functools.partial(reduce_kernel, orders, starts_of(parts, steps)),
        out_shape=[jax.ShapeDtypeStruct(part.shape[1:], jnp.float32) for part in parts],
        in_specs=[vmem] * len(parts),
        out_specs=[vmem] * len(parts),
        scratch_shapes=[
            pltpu.VMEM((2 ** (steps - 1 - k),) + part.shape[1:], part.dtype)
            for part in parts
            for k in range(steps)
        ]
        + [
            pltpu.SemaphoreType.DMA((len(parts), steps)),
            pltpu.SemaphoreType.DMA((len(parts), steps)),
        ],
        compiler_params=pltpu.CompilerParams(
            collective_id=ident, has_side_effects=True, vmem_limit_bytes=56 * 2**20
        ),
    )(*parts)


def expert_kernel(orders, counts, select_ref, back_ref, router_ref, *refs):
    sources, sets, seq_count = counts
    streams, steps = len(orders), len(orders[0])
    ins = refs[:streams]
    weights_in = refs[streams : streams + 3]
    outs = refs[streams + 3 : 2 * streams + 3]
    weights = refs[2 * streams + 3 : 2 * streams + 6]
    rows_in, rows_out, sem = refs[2 * streams + 6 :]
    experts = weights[0].shape[0]
    width = ins[0].shape[2]
    places = 2**steps

    def copy_of(j, e):
        return pltpu.make_async_copy(weights_in[j].at[e], weights[j].at[e], sem.at[j, e])

    for e in range(experts):
        for j in range(3):
            copy_of(j, e).start()

    def whose(order, p):
        source, column_set = 0, 0
        for k, (axis, bit) in enumerate(order):
            value = (p // 2 ** (steps - 1 - k)) % 2
            if axis == "exp":
                column_set = column_set + value * 2**bit
            else:
                source = source + value * 2**bit * (seq_count if axis == "kv" else 1)
        return source, column_set

    def pick(p, carry):
        for i, order in enumerate(orders):
            source, column_set = whose(order, p)
            rows = jnp.dot(select_ref[source], ins[i][p], preferred_element_type=jnp.float32)
            rows = rows.astype(jnp.bfloat16)
            for e in range(experts):
                rows_in[
                    column_set * streams + i, e, pl.ds(pl.multiple_of(source * CAP, CAP), CAP), :
                ] = rows[e * CAP : (e + 1) * CAP]
        return carry

    lax.fori_loop(0, places, pick, 0)
    blocks = sets * streams
    for e in range(experts):
        for j in range(3):
            copy_of(j, e).wait()
        gate_pre = up_pre = logits = 0.0
        for k in range(blocks):
            cut = slice(k * width, (k + 1) * width)
            rows = rows_in[k, e]
            gate_pre += jnp.dot(rows, weights[0][e, cut, :], preferred_element_type=jnp.float32)
            up_pre += jnp.dot(rows, weights[1][e, cut, :], preferred_element_type=jnp.float32)
            logits += jnp.dot(rows, router_ref[cut, :], preferred_element_type=jnp.float32)
        activity = jax.nn.silu(gate_pre) * up_pre * jax.nn.sigmoid(logits[:, e : e + 1])
        activity = activity.astype(jnp.bfloat16)
        for k in range(blocks):
            cut = slice(k * width, (k + 1) * width)
            part = jnp.dot(activity, weights[2][e, :, cut], preferred_element_type=jnp.float32)
            rows_out[k, :, e * CAP : (e + 1) * CAP, :] = part.astype(jnp.bfloat16).reshape(
                sources, CAP, width
            )

    def combine(p, carry):
        for i, order in enumerate(orders):
            source, column_set = whose(order, p)
            outs[i][p] = jnp.dot(
                back_ref[source],
                rows_out[column_set * streams + i, source],
                preferred_element_type=jnp.float32,
            ).astype(jnp.bfloat16)
        return carry

    lax.fori_loop(0, places, combine, 0)


def expert_sums(parts, orders, chosen, router, weights):
    sources, experts, _, tokens = chosen.shape
    sets = lax.axis_size("exp")
    width = parts[0].shape[2]
    select = chosen.reshape(sources, experts * CAP, tokens)
    vmem = pl.BlockSpec(memory_space=pltpu.VMEM)
    blocks = sets * len(parts)
    flops = 6 * experts * sources * CAP * weights[0].shape[1] * weights[0].shape[2]
    return pl.pallas_call(
        functools.partial(expert_kernel, orders, (sources, sets, lax.axis_size("seq"))),
        out_shape=[jax.ShapeDtypeStruct(part.shape, part.dtype) for part in parts],
        in_specs=[vmem] * (3 + len(parts)) + [pl.BlockSpec(memory_space=pl.ANY)] * 3,
        out_specs=[vmem] * len(parts),
        scratch_shapes=[pltpu.VMEM(weight.shape, weight.dtype) for weight in weights]
        + [
            pltpu.VMEM((blocks, experts, sources * CAP, width), jnp.bfloat16),
            pltpu.VMEM((blocks, sources, experts * CAP, width), jnp.bfloat16),
            pltpu.SemaphoreType.DMA((3, experts)),
        ],
        compiler_params=pltpu.CompilerParams(vmem_limit_bytes=58 * 2**20),
        cost_estimate=pl.CostEstimate(
            flops=flops, bytes_accessed=3 * weights[0].size * 2, transcendentals=0
        ),
    )(select, jnp.swapaxes(select, 1, 2), router, *parts, *weights)


def bit_axes():
    return [stage for axis in ("kv", "seq", "exp") for stage in bits_of(axis)[::-1]]


def collect_bits(x, order):
    names = bit_axes()
    x = x.reshape((2,) * len(names) + x.shape[1:])
    tail = range(len(names), x.ndim)
    x = jnp.transpose(x, [order.index(stage) for stage in names] + list(tail))
    return x.reshape((2 ** len(names),) + x.shape[len(names) :])


def stream_orders(count):
    kv, seq, exp = bits_of("kv"), bits_of("seq"), bits_of("exp")
    orders = (kv + exp + seq[::-1], kv[:1] + exp + kv[1:] + seq[::-1])
    return [orders[i % 2] for i in range(count)]


def columns_cut(x, width):
    return [x[..., k : k + width] for k in range(0, x.shape[-1], width)]


def ancestry(parents, draft_len):
    positions = jnp.arange(draft_len, dtype=jnp.int32)
    linked = (parents[:, :, None] == positions[None, None, :]).astype(jnp.float32)
    linked = linked + jnp.eye(draft_len, dtype=jnp.float32)[None]
    for doubling in range((draft_len - 1).bit_length()):
        linked = jnp.minimum(
            jnp.einsum("nij,njk->nik", linked, linked, precision=lax.Precision.HIGHEST), 1.0
        )
    return linked


def merge_pair(former, latter):
    new_max = jnp.maximum(former[0], latter[0])
    former_scale = jnp.exp(former[0] - new_max)
    latter_scale = jnp.exp(latter[0] - new_max)
    return (
        new_max,
        former[1] * former_scale + latter[1] * latter_scale,
        former[2] * former_scale[..., None] + latter[2] * latter_scale[..., None],
    )


def local(
    queries,
    draft_kv,
    kv_pool,
    page_table,
    cache_lens,
    parents,
    hidden,
    norm_gain,
    out_proj,
    router,
    routes,
    gate_w,
    up_w,
    down_w,
):
    set_count = lax.axis_size("exp")
    my_set = lax.axis_index("exp")
    req_count, draft_len, feature_width = queries.shape
    head_dim = feature_width // H
    head_share = H // set_count
    page_count = page_table.shape[1]
    page_len = kv_pool.shape[2]
    draft_share = draft_kv.shape[2]
    slot_ids = jnp.arange(page_count, dtype=jnp.int32)
    page_of = jnp.sum(
        jnp.where(page_table[:, :, 0][:, :, None] == slot_ids, slot_ids[None, :, None], 0), axis=1
    )
    cache_keys = kv_pool[0].reshape(req_count, page_count * page_len, feature_width)
    cache_values = kv_pool[1].reshape(req_count, page_count * page_len, feature_width)
    positions = (
        (page_of * set_count + my_set)[:, :, None] * page_len
        + jnp.arange(page_len, dtype=jnp.int32)[None, None, :]
    ).reshape(req_count, -1)
    cache_seen = positions < cache_lens[:, None]
    linked = ancestry(parents, draft_len)
    draft_seen = lax.dynamic_slice_in_dim(linked, my_set * draft_share, draft_share, 2) > 0.5
    visible = jnp.concatenate(
        [
            jnp.broadcast_to(cache_seen[:, None, :], (req_count, draft_len, page_count * page_len)),
            draft_seen,
        ],
        axis=2,
    )
    key_rows = jnp.concatenate([cache_keys, draft_kv[0]], axis=1).reshape(
        req_count, -1, H, head_dim
    )
    value_rows = jnp.concatenate([cache_values, draft_kv[1]], axis=1).reshape(
        req_count, -1, H, head_dim
    )
    query_rows = queries.reshape(req_count, draft_len, H, head_dim)
    scores = jnp.einsum(
        "rqhd,rkhd->rhqk", query_rows, key_rows, preferred_element_type=jnp.float32
    ) * head_dim ** (-0.5)
    scores = jnp.where(visible[:, None], scores, NEG_FILL)
    row_max = jnp.max(scores, axis=3)
    weights = jnp.where(visible[:, None], jnp.exp(scores - row_max[..., None]), 0.0)
    row_sum = jnp.sum(weights, axis=3)
    weighted = jnp.einsum(
        "rhqk,rkhd->rqhd",
        weights.astype(jnp.bfloat16),
        value_rows,
        preferred_element_type=jnp.float32,
    )
    row_max = jnp.transpose(row_max, (0, 2, 1))
    row_sum = jnp.transpose(row_sum, (0, 2, 1))
    token_rows = req_count * draft_len
    column_count = D // set_count
    exp_bits = bits_of("exp")
    stats = jnp.concatenate([row_max, row_sum], axis=2).reshape(token_rows, 2 * H)
    stats = jnp.pad(stats, ((0, 0), (0, 128 - 2 * H)))
    all_weighted, all_stats = gather_all(
        [weighted.astype(jnp.bfloat16).reshape(token_rows, D), stats], [exp_bits, exp_bits], 1
    )

    def one_set(k):
        return (
            all_stats[k, :, :H].reshape(row_max.shape),
            all_stats[k, :, H : 2 * H].reshape(row_sum.shape),
            all_weighted[k].astype(jnp.float32).reshape(weighted.shape),
        )

    row_max, row_sum, weighted = functools.reduce(
        merge_pair, [one_set(k) for k in range(set_count)]
    )
    attended = (weighted / row_sum[..., None]).astype(jnp.bfloat16)
    attended = lax.dynamic_slice_in_dim(attended, my_set * head_share, head_share, 2)
    attended = attended.reshape(token_rows, head_share * head_dim)
    partial_value = jnp.dot(attended, out_proj, preferred_element_type=jnp.float32)
    by_columns = jnp.transpose(
        partial_value.astype(jnp.bfloat16).reshape(token_rows, set_count, column_count), (1, 0, 2)
    )
    (projected,) = reduce_all([by_columns], [exp_bits[::-1]], 2)

    def own_part(x):
        return lax.dynamic_slice_in_dim(x, my_set * column_count, column_count, x.ndim - 1)

    residual = own_part(hidden.reshape(token_rows, D)).astype(jnp.float32) + projected
    own_sq = jnp.sum(residual * residual, axis=1, keepdims=True)
    (all_sq,) = gather_all([jnp.broadcast_to(own_sq, (token_rows, 128))], [exp_bits], 3)
    mean_sq = jnp.sum(all_sq[:, :, :1], axis=0) / D
    normed = (
        residual * lax.rsqrt(mean_sq + EPS_NORM) * own_part(norm_gain).astype(jnp.float32)[None, :]
    ).astype(jnp.bfloat16)
    width = max(128, column_count // 4)
    streams = column_count // width
    orders = stream_orders(streams)
    local_experts = gate_w.shape[0]
    my_block = lax.axis_index("kv") * lax.axis_size("seq") + lax.axis_index("seq")
    routes_row = jnp.pad(
        jnp.transpose(routes.reshape(token_rows, TOPK)), ((0, 0), (0, -token_rows % 128))
    )
    gathered = gather_all(
        columns_cut(normed, width) + [routes_row],
        [order[::-1] for order in orders] + [orders[0][::-1]],
        4,
    )
    sources = lax.axis_size("kv") * lax.axis_size("seq")
    all_routes = collect_bits(gathered[-1], orders[0]).reshape(
        (sources, set_count) + routes_row.shape
    )[:, 0, :, :token_rows]
    all_routes = jnp.transpose(all_routes, (0, 2, 1))
    expert_ids = my_block * local_experts + jnp.arange(local_experts, dtype=jnp.int32)
    member = jnp.any(all_routes[:, None] == expert_ids[None, :, None, None], axis=3).astype(jnp.int32)
    rank = jnp.cumsum(member, axis=2) - member
    chosen = (member[:, :, None, :] > 0) & (
        rank[:, :, None, :] == jnp.arange(CAP, dtype=jnp.int32)[None, None, :, None]
    )
    chosen = chosen.astype(jnp.bfloat16)
    own_router = lax.dynamic_slice_in_dim(router, my_block * local_experts, local_experts, 1)
    own_router = jnp.pad(own_router, ((0, 0), (0, 128 - local_experts)))
    combined = expert_sums(gathered[:-1], orders, chosen, own_router, (gate_w, up_w, down_w))
    summed_share = jnp.concatenate(reduce_all(combined, orders, 5), axis=1)
    return (
        (residual + summed_share)
        .astype(jnp.bfloat16)
        .reshape(req_count, draft_len, column_count)
    )


def solution(mesh):
    in_specs = (
        P(("kv", "seq"), None, None),
        P(None, ("kv", "seq"), "exp", None),
        P(None, ("kv", "seq", "exp"), None, None),
        P(("kv", "seq"), None, "exp"),
        P(("kv", "seq")),
        P(("kv", "seq"), None),
        P(("kv", "seq"), None, None),
        P(),
        P("exp", None),
        P(),
        P(("kv", "seq"), None, None),
        P(("kv", "seq"), None, "exp"),
        P(("kv", "seq"), None, "exp"),
        P(("kv", "seq"), "exp", None),
    )
    out_specs = P(("kv", "seq"), None, "exp")
    return jax.shard_map(local, mesh=mesh, in_specs=in_specs, out_specs=out_specs, check_vma=False)
```

```python
import functools

import jax
import jax.numpy as jnp
from jax import lax
from jax.experimental import pallas as pl
from jax.experimental.pallas import tpu as pltpu
from jax.sharding import PartitionSpec as P

D = 2048
H = 16
EXPERTS = 64
TOPK = 8
CAP = 16


NEG_FILL = -1e30
EPS_NORM = 1e-06


MESH = pl.DeviceIdType.MESH


def bits_of(axis):
    return [(axis, bit) for bit in range((lax.axis_size(axis) - 1).bit_length())]


def my_bit(stage):
    axis, bit = stage
    return (lax.axis_index(axis) // 2**bit) % 2


def partner(stage):
    axis, bit = stage
    return {axis: lax.axis_index(axis) + (1 - 2 * my_bit(stage)) * 2**bit}


def starts_of(parts, steps):
    if steps < 3:
        return [0] * len(parts)
    return [2 if i in (2, 3) else 0 for i in range(len(parts))]


def greet(stages):
    barrier = pltpu.get_barrier_semaphore()
    for stage in stages:
        pl.semaphore_signal(barrier, inc=1, device_id=partner(stage), device_id_type=MESH)
    pl.semaphore_wait(barrier, len(stages))


def gather_kernel(orders, starts, *refs):
    count = len(orders)
    ins, outs = refs[:count], refs[count : 2 * count]
    send_sem, recv_sem = refs[2 * count :]
    for i, order in enumerate(orders):
        place = sum(my_bit(stage) * 2**k for k, stage in enumerate(order))
        outs[i][place] = ins[i][...]
    greet(sorted(orders[0]))
    copies = [[] for order in orders]
    for slot in range(len(orders[0]) + max(starts)):
        for i, order in enumerate(orders):
            k = slot - starts[i]
            if k < 0 or k > len(order):
                continue
            if k > 0:
                copies[i][k - 1].wait_recv()
            if k == len(order):
                continue
            base = sum(my_bit(stage) * 2**j for j, stage in enumerate(order) if j >= k)
            region = outs[i].at[pl.ds(base, 2**k)]
            copy = pltpu.make_async_remote_copy(
                src_ref=region,
                dst_ref=region,
                send_sem=send_sem.at[i, k],
                recv_sem=recv_sem.at[i, k],
                device_id=partner(order[k]),
                device_id_type=MESH,
            )
            copy.start()
            copies[i].append(copy)
    for i, order in enumerate(orders):
        if starts[i] == max(starts):
            copies[i][-1].wait_recv()
    for i in range(count):
        for copy in copies[i]:
            copy.wait_send()


def gather_all(parts, orders, ident):
    steps = len(orders[0])
    vmem = pl.BlockSpec(memory_space=pltpu.VMEM)
    return pl.pallas_call(
        functools.partial(gather_kernel, orders, starts_of(parts, steps)),
        out_shape=[jax.ShapeDtypeStruct((2**steps,) + part.shape, part.dtype) for part in parts],
        in_specs=[vmem] * len(parts),
        out_specs=[vmem] * len(parts),
        scratch_shapes=[
            pltpu.SemaphoreType.DMA((len(parts), steps)),
            pltpu.SemaphoreType.DMA((len(parts), steps)),
        ],
        compiler_params=pltpu.CompilerParams(
            collective_id=ident, has_side_effects=True, vmem_limit_bytes=56 * 2**20
        ),
    )(*parts)


def reduce_kernel(orders, starts, *refs):
    count, steps = len(orders), len(orders[0])
    ins, outs = refs[:count], refs[count : 2 * count]
    buffers = refs[2 * count : 2 * count + count * steps]
    send_sem, recv_sem = refs[2 * count + count * steps :]
    greet(sorted(orders[0]))
    copies = [[] for order in orders]

    def held(i, k):
        return ins[i] if k == 0 else buffers[i * steps + k - 1]

    def add_in(i, k):
        half = 2 ** (steps - 1 - k)
        base = my_bit(orders[i][k]) * half
        mine, came = held(i, k), buffers[i * steps + k]

        def one(j, carry):
            total = mine[base + j].astype(jnp.float32) + came[j].astype(jnp.float32)
            if k == steps - 1:
                outs[i][...] = total
            else:
                came[j] = total.astype(came.dtype)
            return carry

        lax.fori_loop(0, half, one, 0)

    for slot in range(steps + max(starts)):
        for i, order in enumerate(orders):
            k = slot - starts[i]
            if k < 0 or k > steps:
                continue
            if k > 0:
                copies[i][k - 1].wait_recv()
                add_in(i, k - 1)
            if k == steps:
                continue
            half = 2 ** (steps - 1 - k)
            copy = pltpu.make_async_remote_copy(
                src_ref=held(i, k).at[pl.ds((1 - my_bit(order[k])) * half, half)],
                dst_ref=buffers[i * steps + k],
                send_sem=send_sem.at[i, k],
                recv_sem=recv_sem.at[i, k],
                device_id=partner(order[k]),
                device_id_type=MESH,
            )
            copy.start()
            copies[i].append(copy)
    for i in range(count):
        if starts[i] == max(starts):
            copies[i][-1].wait_recv()
            add_in(i, steps - 1)
    for i in range(count):
        for copy in copies[i]:
            copy.wait_send()


def reduce_all(parts, orders, ident):
    steps = len(orders[0])
    vmem = pl.BlockSpec(memory_space=pltpu.VMEM)
    return pl.pallas_call(
        functools.partial(reduce_kernel, orders, [0] * len(parts)),
        out_shape=[jax.ShapeDtypeStruct(part.shape[1:], jnp.float32) for part in parts],
        in_specs=[vmem] * len(parts),
        out_specs=[vmem] * len(parts),
        scratch_shapes=[
            pltpu.VMEM((2 ** (steps - 1 - k),) + part.shape[1:], part.dtype)
            for part in parts
            for k in range(steps)
        ]
        + [
            pltpu.SemaphoreType.DMA((len(parts), steps)),
            pltpu.SemaphoreType.DMA((len(parts), steps)),
        ],
        compiler_params=pltpu.CompilerParams(
            collective_id=ident, has_side_effects=True, vmem_limit_bytes=56 * 2**20
        ),
    )(*parts)


def expert_kernel(orders, counts, select_ref, back_ref, norm_ref, router_ref, *refs):
    sources, sets, seq_count = counts
    streams, steps = len(orders), len(orders[0])
    ins = refs[:streams]
    weights_in = refs[streams : streams + 3]
    outs = refs[streams + 3 : 2 * streams + 3]
    weights = refs[2 * streams + 3 : 2 * streams + 6]
    rows_in, rows_out, sem = refs[2 * streams + 6 :]
    experts = weights[0].shape[0]
    width = ins[0].shape[2]
    places = 2**steps

    def copy_of(j, e):
        return pltpu.make_async_copy(weights_in[j].at[e], weights[j].at[e], sem.at[j, e])

    for e in range(experts):
        for j in range(3):
            copy_of(j, e).start()

    def whose(order, p):
        source, column_set = 0, 0
        for k, (axis, bit) in enumerate(order):
            value = (p // 2 ** (steps - 1 - k)) % 2
            if axis == "exp":
                column_set = column_set + value * 2**bit
            else:
                source = source + value * 2**bit * (seq_count if axis == "kv" else 1)
        return source, column_set

    def pick(p, carry):
        for i, order in enumerate(orders):
            source, column_set = whose(order, p)
            rows = jnp.dot(select_ref[source], ins[i][p], preferred_element_type=jnp.float32)
            rows = rows.astype(jnp.bfloat16)
            for e in range(experts):
                rows_in[
                    column_set * streams + i, e, pl.ds(pl.multiple_of(source * CAP, CAP), CAP), :
                ] = rows[e * CAP : (e + 1) * CAP]
        return carry

    lax.fori_loop(0, places, pick, 0)
    blocks = sets * streams
    for e in range(experts):
        for j in range(3):
            copy_of(j, e).wait()
        gate_pre = up_pre = logits = 0.0
        for k in range(blocks):
            cut = slice(k * width, (k + 1) * width)
            rows = rows_in[k, e]
            gate_pre += jnp.dot(rows, weights[0][e, cut, :], preferred_element_type=jnp.float32)
            up_pre += jnp.dot(rows, weights[1][e, cut, :], preferred_element_type=jnp.float32)
            logits += jnp.dot(rows, router_ref[cut, :], preferred_element_type=jnp.float32)
        norm = norm_ref[e]
        gate = jax.nn.sigmoid(logits[:, e : e + 1] * norm)
        activity = jax.nn.silu(gate_pre * norm) * (up_pre * norm) * gate
        activity = activity.astype(jnp.bfloat16)
        for k in range(blocks):
            cut = slice(k * width, (k + 1) * width)
            part = jnp.dot(activity, weights[2][e, :, cut], preferred_element_type=jnp.float32)
            rows_out[k, :, e * CAP : (e + 1) * CAP, :] = part.astype(jnp.bfloat16).reshape(
                sources, CAP, width
            )

    def combine(p, carry):
        for i, order in enumerate(orders):
            source, column_set = whose(order, p)
            outs[i][p] = jnp.dot(
                back_ref[source],
                rows_out[column_set * streams + i, source],
                preferred_element_type=jnp.float32,
            ).astype(jnp.bfloat16)
        return carry

    lax.fori_loop(0, places, combine, 0)


def expert_sums(parts, orders, chosen, slot_norm, router, weights):
    sources, experts, _, tokens = chosen.shape
    sets = lax.axis_size("exp")
    width = parts[0].shape[2]
    select = chosen.reshape(sources, experts * CAP, tokens)
    vmem = pl.BlockSpec(memory_space=pltpu.VMEM)
    blocks = sets * len(parts)
    flops = 6 * experts * sources * CAP * weights[0].shape[1] * weights[0].shape[2]
    return pl.pallas_call(
        functools.partial(expert_kernel, orders, (sources, sets, lax.axis_size("seq"))),
        out_shape=[jax.ShapeDtypeStruct(part.shape, part.dtype) for part in parts],
        in_specs=[vmem] * (4 + len(parts)) + [pl.BlockSpec(memory_space=pl.ANY)] * 3,
        out_specs=[vmem] * len(parts),
        scratch_shapes=[pltpu.VMEM(weight.shape, weight.dtype) for weight in weights]
        + [
            pltpu.VMEM((blocks, experts, sources * CAP, width), jnp.bfloat16),
            pltpu.VMEM((blocks, sources, experts * CAP, width), jnp.bfloat16),
            pltpu.SemaphoreType.DMA((3, experts)),
        ],
        compiler_params=pltpu.CompilerParams(vmem_limit_bytes=58 * 2**20),
        cost_estimate=pl.CostEstimate(
            flops=flops, bytes_accessed=3 * weights[0].size * 2, transcendentals=0
        ),
    )(select, jnp.swapaxes(select, 1, 2), slot_norm, router, *parts, *weights)


def bit_axes():
    return [stage for axis in ("kv", "seq", "exp") for stage in bits_of(axis)[::-1]]


def collect_bits(x, order):
    names = bit_axes()
    x = x.reshape((2,) * len(names) + x.shape[1:])
    tail = range(len(names), x.ndim)
    x = jnp.transpose(x, [order.index(stage) for stage in names] + list(tail))
    return x.reshape((2 ** len(names),) + x.shape[len(names) :])


def stream_orders(count):
    kv, seq, exp = bits_of("kv"), bits_of("seq"), bits_of("exp")
    orders = (kv + exp + seq[::-1], kv[:1] + exp + kv[1:] + seq[::-1])
    return [orders[i % 2] for i in range(count)]


def columns_cut(x, width):
    return [x[..., k : k + width] for k in range(0, x.shape[-1], width)]


def ancestry(parents, draft_len):
    positions = jnp.arange(draft_len, dtype=jnp.int32)
    linked = (parents[:, :, None] == positions[None, None, :]).astype(jnp.float32)
    linked = linked + jnp.eye(draft_len, dtype=jnp.float32)[None]
    for doubling in range((draft_len - 1).bit_length()):
        linked = jnp.minimum(
            jnp.einsum("nij,njk->nik", linked, linked, precision=lax.Precision.HIGHEST), 1.0
        )
    return linked


def merge_pair(former, latter):
    new_max = jnp.maximum(former[0], latter[0])
    former_scale = jnp.exp(former[0] - new_max)
    latter_scale = jnp.exp(latter[0] - new_max)
    return (
        new_max,
        former[1] * former_scale + latter[1] * latter_scale,
        former[2] * former_scale[..., None] + latter[2] * latter_scale[..., None],
    )


def local(
    queries,
    draft_kv,
    kv_pool,
    page_table,
    cache_lens,
    parents,
    hidden,
    norm_gain,
    out_proj,
    router,
    routes,
    gate_w,
    up_w,
    down_w,
):
    set_count = lax.axis_size("exp")
    my_set = lax.axis_index("exp")
    req_count, draft_len, feature_width = queries.shape
    head_dim = feature_width // H
    head_share = H // set_count
    page_count = page_table.shape[1]
    page_len = kv_pool.shape[2]
    draft_share = draft_kv.shape[2]
    slot_ids = jnp.arange(page_count, dtype=jnp.int32)
    page_of = jnp.sum(
        jnp.where(page_table[:, :, 0][:, :, None] == slot_ids, slot_ids[None, :, None], 0), axis=1
    )
    cache_keys = kv_pool[0].reshape(req_count, page_count * page_len, feature_width)
    cache_values = kv_pool[1].reshape(req_count, page_count * page_len, feature_width)
    positions = (
        (page_of * set_count + my_set)[:, :, None] * page_len
        + jnp.arange(page_len, dtype=jnp.int32)[None, None, :]
    ).reshape(req_count, -1)
    cache_seen = positions < cache_lens[:, None]
    linked = ancestry(parents, draft_len)
    draft_seen = lax.dynamic_slice_in_dim(linked, my_set * draft_share, draft_share, 2) > 0.5
    visible = jnp.concatenate(
        [
            jnp.broadcast_to(cache_seen[:, None, :], (req_count, draft_len, page_count * page_len)),
            draft_seen,
        ],
        axis=2,
    )
    key_rows = jnp.concatenate([cache_keys, draft_kv[0]], axis=1).reshape(
        req_count, -1, H, head_dim
    )
    value_rows = jnp.concatenate([cache_values, draft_kv[1]], axis=1).reshape(
        req_count, -1, H, head_dim
    )
    query_rows = queries.reshape(req_count, draft_len, H, head_dim)
    scores = jnp.einsum(
        "rqhd,rkhd->rhqk", query_rows, key_rows, preferred_element_type=jnp.float32
    ) * head_dim ** (-0.5)
    scores = jnp.where(visible[:, None], scores, NEG_FILL)
    row_max = jnp.max(scores, axis=3)
    weights = jnp.where(visible[:, None], jnp.exp(scores - row_max[..., None]), 0.0)
    row_sum = jnp.sum(weights, axis=3)
    weighted = jnp.einsum(
        "rhqk,rkhd->rqhd",
        weights.astype(jnp.bfloat16),
        value_rows,
        preferred_element_type=jnp.float32,
    )
    row_max = jnp.transpose(row_max, (0, 2, 1))
    row_sum = jnp.transpose(row_sum, (0, 2, 1))
    token_rows = req_count * draft_len
    column_count = D // set_count
    exp_bits = bits_of("exp")
    stats = jnp.concatenate([row_max, row_sum], axis=2).reshape(token_rows, 2 * H)
    stats = jnp.pad(stats, ((0, 0), (0, 128 - 2 * H)))
    all_weighted, all_stats = gather_all(
        [weighted.astype(jnp.bfloat16).reshape(token_rows, D), stats], [exp_bits, exp_bits], 1
    )

    def one_set(k):
        return (
            all_stats[k, :, :H].reshape(row_max.shape),
            all_stats[k, :, H : 2 * H].reshape(row_sum.shape),
            all_weighted[k].astype(jnp.float32).reshape(weighted.shape),
        )

    row_max, row_sum, weighted = functools.reduce(
        merge_pair, [one_set(k) for k in range(set_count)]
    )
    attended = (weighted / row_sum[..., None]).astype(jnp.bfloat16)
    attended = lax.dynamic_slice_in_dim(attended, my_set * head_share, head_share, 2)
    attended = attended.reshape(token_rows, head_share * head_dim)
    partial_value = jnp.dot(attended, out_proj, preferred_element_type=jnp.float32)
    by_columns = jnp.transpose(
        partial_value.astype(jnp.bfloat16).reshape(token_rows, set_count, column_count), (1, 0, 2)
    )
    (projected,) = reduce_all([by_columns], [exp_bits[::-1]], 2)

    def own_part(x):
        return lax.dynamic_slice_in_dim(x, my_set * column_count, column_count, x.ndim - 1)

    residual = own_part(hidden.reshape(token_rows, D)).astype(jnp.float32) + projected
    own_sq = jnp.sum(residual * residual, axis=1, keepdims=True)
    weighed = (residual * own_part(norm_gain).astype(jnp.float32)[None, :]).astype(jnp.bfloat16)
    width = max(128, column_count // 4)
    streams = column_count // width
    orders = stream_orders(streams)
    local_experts = gate_w.shape[0]
    my_block = lax.axis_index("kv") * lax.axis_size("seq") + lax.axis_index("seq")
    routes_row = jnp.pad(
        jnp.transpose(routes.reshape(token_rows, TOPK)), ((0, 0), (0, -token_rows % 128))
    )
    sq_row = jnp.pad(jnp.transpose(own_sq), ((0, 7), (0, -token_rows % 128)))
    gathered = gather_all(
        columns_cut(weighed, width) + [routes_row, sq_row],
        [order[::-1] for order in orders] + [orders[0][::-1]] * 2,
        4,
    )
    sources = lax.axis_size("kv") * lax.axis_size("seq")
    all_sq = collect_bits(gathered[-1], orders[0]).reshape((sources, set_count) + sq_row.shape)
    mean_sq = jnp.sum(all_sq[:, :, 0, :token_rows], axis=1) / D
    inverse_norm = lax.rsqrt(mean_sq + EPS_NORM)
    all_routes = collect_bits(gathered[-2], orders[0]).reshape(
        (sources, set_count) + routes_row.shape
    )[:, 0, :, :token_rows]
    all_routes = jnp.transpose(all_routes, (0, 2, 1))
    expert_ids = my_block * local_experts + jnp.arange(local_experts, dtype=jnp.int32)
    member = jnp.any(all_routes[:, None] == expert_ids[None, :, None, None], axis=3).astype(jnp.int32)
    rank = jnp.cumsum(member, axis=2) - member
    chosen = (member[:, :, None, :] > 0) & (
        rank[:, :, None, :] == jnp.arange(CAP, dtype=jnp.int32)[None, None, :, None]
    )
    slot_norm = jnp.sum(jnp.where(chosen, inverse_norm[:, None, None, :], 0.0), axis=3)
    slot_norm = jnp.transpose(slot_norm, (1, 0, 2)).reshape(local_experts, sources * CAP, 1)
    chosen = chosen.astype(jnp.bfloat16)
    own_router = lax.dynamic_slice_in_dim(router, my_block * local_experts, local_experts, 1)
    own_router = jnp.pad(own_router, ((0, 0), (0, 128 - local_experts)))
    combined = expert_sums(gathered[:-2], orders, chosen, slot_norm, own_router, (gate_w, up_w, down_w))
    summed_share = jnp.concatenate(reduce_all(combined, orders, 5), axis=1)
    return (
        (residual + summed_share)
        .astype(jnp.bfloat16)
        .reshape(req_count, draft_len, column_count)
    )


def solution(mesh):
    in_specs = (
        P(("kv", "seq"), None, None),
        P(None, ("kv", "seq"), "exp", None),
        P(None, ("kv", "seq", "exp"), None, None),
        P(("kv", "seq"), None, "exp"),
        P(("kv", "seq")),
        P(("kv", "seq"), None),
        P(("kv", "seq"), None, None),
        P(),
        P("exp", None),
        P(),
        P(("kv", "seq"), None, None),
        P(("kv", "seq"), None, "exp"),
        P(("kv", "seq"), None, "exp"),
        P(("kv", "seq"), "exp", None),
    )
    out_specs = P(("kv", "seq"), None, "exp")
    return jax.shard_map(local, mesh=mesh, in_specs=in_specs, out_specs=out_specs, check_vma=False)
```

```python
import functools

import jax
import jax.numpy as jnp
from jax import lax
from jax.experimental import pallas as pl
from jax.experimental.pallas import tpu as pltpu
from jax.sharding import PartitionSpec as P

D = 2048
H = 16
EXPERTS = 64
TOPK = 8
CAP = 16


NEG_FILL = -1e30
EPS_NORM = 1e-06


MESH = pl.DeviceIdType.MESH


def bits_of(axis):
    return [(axis, bit) for bit in range((lax.axis_size(axis) - 1).bit_length())]


def my_bit(stage):
    axis, bit = stage
    return (lax.axis_index(axis) // 2**bit) % 2


def partner(stage):
    axis, bit = stage
    return {axis: lax.axis_index(axis) + (1 - 2 * my_bit(stage)) * 2**bit}


def starts_of(parts, steps):
    if steps < 3:
        return [0] * len(parts)
    return [2 if i in (2, 3) else 0 for i in range(len(parts))]


def greet(stages):
    barrier = pltpu.get_barrier_semaphore()
    for stage in stages:
        pl.semaphore_signal(barrier, inc=1, device_id=partner(stage), device_id_type=MESH)
    pl.semaphore_wait(barrier, len(stages))


def gather_kernel(orders, starts, *refs):
    count = len(orders)
    ins, outs = refs[:count], refs[count : 2 * count]
    send_sem, recv_sem = refs[2 * count :]
    for i, order in enumerate(orders):
        place = sum(my_bit(stage) * 2**k for k, stage in enumerate(order))
        outs[i][place] = ins[i][...]
    greet(sorted(orders[0]))
    copies = [[] for order in orders]
    for slot in range(len(orders[0]) + max(starts)):
        for i, order in enumerate(orders):
            k = slot - starts[i]
            if k < 0 or k > len(order):
                continue
            if k > 0:
                copies[i][k - 1].wait_recv()
            if k == len(order):
                continue
            base = sum(my_bit(stage) * 2**j for j, stage in enumerate(order) if j >= k)
            region = outs[i].at[pl.ds(base, 2**k)]
            copy = pltpu.make_async_remote_copy(
                src_ref=region,
                dst_ref=region,
                send_sem=send_sem.at[i, k],
                recv_sem=recv_sem.at[i, k],
                device_id=partner(order[k]),
                device_id_type=MESH,
            )
            copy.start()
            copies[i].append(copy)
    for i, order in enumerate(orders):
        if starts[i] == max(starts):
            copies[i][-1].wait_recv()
    for i in range(count):
        for copy in copies[i]:
            copy.wait_send()


def gather_all(parts, orders, ident):
    steps = len(orders[0])
    vmem = pl.BlockSpec(memory_space=pltpu.VMEM)
    return pl.pallas_call(
        functools.partial(gather_kernel, orders, starts_of(parts, steps)),
        out_shape=[jax.ShapeDtypeStruct((2**steps,) + part.shape, part.dtype) for part in parts],
        in_specs=[vmem] * len(parts),
        out_specs=[vmem] * len(parts),
        scratch_shapes=[
            pltpu.SemaphoreType.DMA((len(parts), steps)),
            pltpu.SemaphoreType.DMA((len(parts), steps)),
        ],
        compiler_params=pltpu.CompilerParams(
            collective_id=ident, has_side_effects=True, vmem_limit_bytes=56 * 2**20
        ),
    )(*parts)


def reduce_kernel(orders, starts, *refs):
    count, steps = len(orders), len(orders[0])
    ins, outs = refs[:count], refs[count : 2 * count]
    buffers = refs[2 * count : 2 * count + count * steps]
    send_sem, recv_sem = refs[2 * count + count * steps :]
    greet(sorted(orders[0]))
    copies = [[] for order in orders]

    def held(i, k):
        return ins[i] if k == 0 else buffers[i * steps + k - 1]

    def add_in(i, k):
        half = 2 ** (steps - 1 - k)
        base = my_bit(orders[i][k]) * half
        mine, came = held(i, k), buffers[i * steps + k]

        def one(j, carry):
            total = mine[base + j].astype(jnp.float32) + came[j].astype(jnp.float32)
            if k == steps - 1:
                outs[i][...] = total
            else:
                came[j] = total.astype(came.dtype)
            return carry

        lax.fori_loop(0, half, one, 0)

    for slot in range(steps + max(starts)):
        for i, order in enumerate(orders):
            k = slot - starts[i]
            if k < 0 or k > steps:
                continue
            if k > 0:
                copies[i][k - 1].wait_recv()
                add_in(i, k - 1)
            if k == steps:
                continue
            half = 2 ** (steps - 1 - k)
            copy = pltpu.make_async_remote_copy(
                src_ref=held(i, k).at[pl.ds((1 - my_bit(order[k])) * half, half)],
                dst_ref=buffers[i * steps + k],
                send_sem=send_sem.at[i, k],
                recv_sem=recv_sem.at[i, k],
                device_id=partner(order[k]),
                device_id_type=MESH,
            )
            copy.start()
            copies[i].append(copy)
    for i in range(count):
        if starts[i] == max(starts):
            copies[i][-1].wait_recv()
            add_in(i, steps - 1)
    for i in range(count):
        for copy in copies[i]:
            copy.wait_send()


def reduce_all(parts, orders, ident):
    steps = len(orders[0])
    vmem = pl.BlockSpec(memory_space=pltpu.VMEM)
    return pl.pallas_call(
        functools.partial(reduce_kernel, orders, [0] * len(parts)),
        out_shape=[jax.ShapeDtypeStruct(part.shape[1:], jnp.float32) for part in parts],
        in_specs=[vmem] * len(parts),
        out_specs=[vmem] * len(parts),
        scratch_shapes=[
            pltpu.VMEM((2 ** (steps - 1 - k),) + part.shape[1:], part.dtype)
            for part in parts
            for k in range(steps)
        ]
        + [
            pltpu.SemaphoreType.DMA((len(parts), steps)),
            pltpu.SemaphoreType.DMA((len(parts), steps)),
        ],
        compiler_params=pltpu.CompilerParams(
            collective_id=ident, has_side_effects=True, vmem_limit_bytes=56 * 2**20
        ),
    )(*parts)


def expert_kernel(orders, counts, select_ref, back_ref, norm_ref, router_ref, *refs):
    sources, sets, seq_count = counts
    streams, steps = len(orders), len(orders[0])
    ins = refs[:streams]
    weights_in = refs[streams : streams + 3]
    outs = refs[streams + 3 : 2 * streams + 3]
    weights = refs[2 * streams + 3 : 2 * streams + 6]
    rows_in, rows_out, sem = refs[2 * streams + 6 :]
    experts = weights[0].shape[0]
    width = ins[0].shape[2]
    places = 2**steps

    def copy_of(j, e):
        return pltpu.make_async_copy(weights_in[j].at[e], weights[j].at[e], sem.at[j, e])

    for e in range(experts):
        for j in range(3):
            copy_of(j, e).start()

    def whose(order, p):
        source, column_set = 0, 0
        for k, (axis, bit) in enumerate(order):
            value = (p // 2 ** (steps - 1 - k)) % 2
            if axis == "exp":
                column_set = column_set + value * 2**bit
            else:
                source = source + value * 2**bit * (seq_count if axis == "kv" else 1)
        return source, column_set

    def in_fours(body):
        def four(quarter, carry):
            for step in range(4):
                carry = body(quarter * 4 + step, carry)
            return carry

        lax.fori_loop(0, places // 4, four, 0)

    def pick(p, carry):
        for i, order in enumerate(orders):
            source, column_set = whose(order, p)
            rows = jnp.dot(select_ref[source], ins[i][p], preferred_element_type=jnp.float32)
            rows = rows.astype(jnp.bfloat16)
            for e in range(experts):
                rows_in[
                    column_set * streams + i, e, pl.ds(pl.multiple_of(source * CAP, CAP), CAP), :
                ] = rows[e * CAP : (e + 1) * CAP]
        return carry

    in_fours(pick)
    blocks = sets * streams
    for e in range(experts):
        for j in range(3):
            copy_of(j, e).wait()
        gate_pre = up_pre = logits = 0.0
        for k in range(blocks):
            cut = slice(k * width, (k + 1) * width)
            rows = rows_in[k, e]
            gate_pre += jnp.dot(rows, weights[0][e, cut, :], preferred_element_type=jnp.float32)
            up_pre += jnp.dot(rows, weights[1][e, cut, :], preferred_element_type=jnp.float32)
            logits += jnp.dot(rows, router_ref[cut, :], preferred_element_type=jnp.float32)
        norm = norm_ref[e]
        gate = jax.nn.sigmoid(logits[:, e : e + 1] * norm)
        activity = jax.nn.silu(gate_pre * norm) * (up_pre * norm) * gate
        activity = activity.astype(jnp.bfloat16)
        for k in range(blocks):
            cut = slice(k * width, (k + 1) * width)
            part = jnp.dot(activity, weights[2][e, :, cut], preferred_element_type=jnp.float32)
            rows_out[k, :, e * CAP : (e + 1) * CAP, :] = part.astype(jnp.bfloat16).reshape(
                sources, CAP, width
            )

    def combine(p, carry):
        for i, order in enumerate(orders):
            source, column_set = whose(order, p)
            outs[i][p] = jnp.dot(
                back_ref[source],
                rows_out[column_set * streams + i, source],
                preferred_element_type=jnp.float32,
            ).astype(jnp.bfloat16)
        return carry

    in_fours(combine)


def expert_sums(parts, orders, chosen, slot_norm, router, weights):
    sources, experts, _, tokens = chosen.shape
    sets = lax.axis_size("exp")
    width = parts[0].shape[2]
    select = chosen.reshape(sources, experts * CAP, tokens)
    vmem = pl.BlockSpec(memory_space=pltpu.VMEM)
    blocks = sets * len(parts)
    flops = 6 * experts * sources * CAP * weights[0].shape[1] * weights[0].shape[2]
    return pl.pallas_call(
        functools.partial(expert_kernel, orders, (sources, sets, lax.axis_size("seq"))),
        out_shape=[jax.ShapeDtypeStruct(part.shape, part.dtype) for part in parts],
        in_specs=[vmem] * (4 + len(parts)) + [pl.BlockSpec(memory_space=pl.ANY)] * 3,
        out_specs=[vmem] * len(parts),
        scratch_shapes=[pltpu.VMEM(weight.shape, weight.dtype) for weight in weights]
        + [
            pltpu.VMEM((blocks, experts, sources * CAP, width), jnp.bfloat16),
            pltpu.VMEM((blocks, sources, experts * CAP, width), jnp.bfloat16),
            pltpu.SemaphoreType.DMA((3, experts)),
        ],
        compiler_params=pltpu.CompilerParams(vmem_limit_bytes=58 * 2**20),
        cost_estimate=pl.CostEstimate(
            flops=flops, bytes_accessed=3 * weights[0].size * 2, transcendentals=0
        ),
    )(select, jnp.swapaxes(select, 1, 2), slot_norm, router, *parts, *weights)


def bit_axes():
    return [stage for axis in ("kv", "seq", "exp") for stage in bits_of(axis)[::-1]]


def collect_bits(x, order):
    names = bit_axes()
    x = x.reshape((2,) * len(names) + x.shape[1:])
    tail = range(len(names), x.ndim)
    x = jnp.transpose(x, [order.index(stage) for stage in names] + list(tail))
    return x.reshape((2 ** len(names),) + x.shape[len(names) :])


def stream_orders(count):
    kv, seq, exp = bits_of("kv"), bits_of("seq"), bits_of("exp")
    orders = (kv + exp + seq[::-1], kv[:1] + exp + kv[1:] + seq[::-1])
    return [orders[i % 2] for i in range(count)]


def columns_cut(x, width):
    return [x[..., k : k + width] for k in range(0, x.shape[-1], width)]


def ancestry(parents, draft_len):
    positions = jnp.arange(draft_len, dtype=jnp.int32)
    linked = (parents[:, :, None] == positions[None, None, :]).astype(jnp.float32)
    linked = linked + jnp.eye(draft_len, dtype=jnp.float32)[None]
    for doubling in range((draft_len - 1).bit_length()):
        linked = jnp.minimum(
            jnp.einsum("nij,njk->nik", linked, linked, precision=lax.Precision.HIGHEST), 1.0
        )
    return linked


def merge_pair(former, latter):
    new_max = jnp.maximum(former[0], latter[0])
    former_scale = jnp.exp(former[0] - new_max)
    latter_scale = jnp.exp(latter[0] - new_max)
    return (
        new_max,
        former[1] * former_scale + latter[1] * latter_scale,
        former[2] * former_scale[..., None] + latter[2] * latter_scale[..., None],
    )


def local(
    queries,
    draft_kv,
    kv_pool,
    page_table,
    cache_lens,
    parents,
    hidden,
    norm_gain,
    out_proj,
    router,
    routes,
    gate_w,
    up_w,
    down_w,
):
    set_count = lax.axis_size("exp")
    my_set = lax.axis_index("exp")
    req_count, draft_len, feature_width = queries.shape
    head_dim = feature_width // H
    head_share = H // set_count
    page_count = page_table.shape[1]
    page_len = kv_pool.shape[2]
    draft_share = draft_kv.shape[2]
    slot_ids = jnp.arange(page_count, dtype=jnp.int32)
    page_of = jnp.sum(
        jnp.where(page_table[:, :, 0][:, :, None] == slot_ids, slot_ids[None, :, None], 0), axis=1
    )
    cache_keys = kv_pool[0].reshape(req_count, page_count * page_len, feature_width)
    cache_values = kv_pool[1].reshape(req_count, page_count * page_len, feature_width)
    positions = (
        (page_of * set_count + my_set)[:, :, None] * page_len
        + jnp.arange(page_len, dtype=jnp.int32)[None, None, :]
    ).reshape(req_count, -1)
    cache_seen = positions < cache_lens[:, None]
    linked = ancestry(parents, draft_len)
    draft_seen = lax.dynamic_slice_in_dim(linked, my_set * draft_share, draft_share, 2) > 0.5
    visible = jnp.concatenate(
        [
            jnp.broadcast_to(cache_seen[:, None, :], (req_count, draft_len, page_count * page_len)),
            draft_seen,
        ],
        axis=2,
    )
    key_rows = jnp.concatenate([cache_keys, draft_kv[0]], axis=1).reshape(
        req_count, -1, H, head_dim
    )
    value_rows = jnp.concatenate([cache_values, draft_kv[1]], axis=1).reshape(
        req_count, -1, H, head_dim
    )
    query_rows = queries.reshape(req_count, draft_len, H, head_dim)
    scores = jnp.einsum(
        "rqhd,rkhd->rhqk", query_rows, key_rows, preferred_element_type=jnp.float32
    ) * head_dim ** (-0.5)
    scores = jnp.where(visible[:, None], scores, NEG_FILL)
    row_max = jnp.max(scores, axis=3)
    weights = jnp.where(visible[:, None], jnp.exp(scores - row_max[..., None]), 0.0)
    row_sum = jnp.sum(weights, axis=3)
    weighted = jnp.einsum(
        "rhqk,rkhd->rqhd",
        weights.astype(jnp.bfloat16),
        value_rows,
        preferred_element_type=jnp.float32,
    )
    row_max = jnp.transpose(row_max, (0, 2, 1))
    row_sum = jnp.transpose(row_sum, (0, 2, 1))
    token_rows = req_count * draft_len
    column_count = D // set_count
    exp_bits = bits_of("exp")
    stats = jnp.concatenate([row_max, row_sum], axis=2).reshape(token_rows, 2 * H)
    stats = jnp.pad(stats, ((0, 0), (0, 128 - 2 * H)))
    all_weighted, all_stats = gather_all(
        [weighted.astype(jnp.bfloat16).reshape(token_rows, D), stats], [exp_bits, exp_bits], 1
    )

    def one_set(k):
        return (
            all_stats[k, :, :H].reshape(row_max.shape),
            all_stats[k, :, H : 2 * H].reshape(row_sum.shape),
            all_weighted[k].astype(jnp.float32).reshape(weighted.shape),
        )

    row_max, row_sum, weighted = functools.reduce(
        merge_pair, [one_set(k) for k in range(set_count)]
    )
    attended = (weighted / row_sum[..., None]).astype(jnp.bfloat16)
    attended = lax.dynamic_slice_in_dim(attended, my_set * head_share, head_share, 2)
    attended = attended.reshape(token_rows, head_share * head_dim)
    partial_value = jnp.dot(attended, out_proj, preferred_element_type=jnp.float32)
    by_columns = jnp.transpose(
        partial_value.astype(jnp.bfloat16).reshape(token_rows, set_count, column_count), (1, 0, 2)
    )
    (projected,) = reduce_all([by_columns], [exp_bits[::-1]], 2)

    def own_part(x):
        return lax.dynamic_slice_in_dim(x, my_set * column_count, column_count, x.ndim - 1)

    residual = own_part(hidden.reshape(token_rows, D)).astype(jnp.float32) + projected
    own_sq = jnp.sum(residual * residual, axis=1, keepdims=True)
    weighed = (residual * own_part(norm_gain).astype(jnp.float32)[None, :]).astype(jnp.bfloat16)
    width = max(128, column_count // 4)
    streams = column_count // width
    orders = stream_orders(streams)
    local_experts = gate_w.shape[0]
    my_block = lax.axis_index("kv") * lax.axis_size("seq") + lax.axis_index("seq")
    routes_row = jnp.pad(
        jnp.transpose(routes.reshape(token_rows, TOPK)), ((0, 0), (0, -token_rows % 128))
    )
    sq_row = jnp.pad(jnp.transpose(own_sq), ((0, 7), (0, -token_rows % 128)))
    gathered = gather_all(
        columns_cut(weighed, width) + [routes_row, sq_row],
        [order[::-1] for order in orders] + [orders[0][::-1]] * 2,
        4,
    )
    sources = lax.axis_size("kv") * lax.axis_size("seq")
    all_sq = collect_bits(gathered[-1], orders[0]).reshape((sources, set_count) + sq_row.shape)
    mean_sq = jnp.sum(all_sq[:, :, 0, :token_rows], axis=1) / D
    inverse_norm = lax.rsqrt(mean_sq + EPS_NORM)
    all_routes = collect_bits(gathered[-2], orders[0]).reshape(
        (sources, set_count) + routes_row.shape
    )[:, 0, :, :token_rows]
    all_routes = jnp.transpose(all_routes, (0, 2, 1))
    expert_ids = my_block * local_experts + jnp.arange(local_experts, dtype=jnp.int32)
    member = jnp.any(all_routes[:, None] == expert_ids[None, :, None, None], axis=3).astype(jnp.int32)
    rank = jnp.cumsum(member, axis=2) - member
    chosen = (member[:, :, None, :] > 0) & (
        rank[:, :, None, :] == jnp.arange(CAP, dtype=jnp.int32)[None, None, :, None]
    )
    slot_norm = jnp.sum(jnp.where(chosen, inverse_norm[:, None, None, :], 0.0), axis=3)
    slot_norm = jnp.transpose(slot_norm, (1, 0, 2)).reshape(local_experts, sources * CAP, 1)
    chosen = chosen.astype(jnp.bfloat16)
    own_router = lax.dynamic_slice_in_dim(router, my_block * local_experts, local_experts, 1)
    own_router = jnp.pad(own_router, ((0, 0), (0, 128 - local_experts)))
    combined = expert_sums(gathered[:-2], orders, chosen, slot_norm, own_router, (gate_w, up_w, down_w))
    summed_share = jnp.concatenate(reduce_all(combined, orders, 5), axis=1)
    return (
        (residual + summed_share)
        .astype(jnp.bfloat16)
        .reshape(req_count, draft_len, column_count)
    )


def solution(mesh):
    in_specs = (
        P(("kv", "seq"), None, None),
        P(None, ("kv", "seq"), "exp", None),
        P(None, ("kv", "seq", "exp"), None, None),
        P(("kv", "seq"), None, "exp"),
        P(("kv", "seq")),
        P(("kv", "seq"), None),
        P(("kv", "seq"), None, None),
        P(),
        P("exp", None),
        P(),
        P(("kv", "seq"), None, None),
        P(("kv", "seq"), None, "exp"),
        P(("kv", "seq"), None, "exp"),
        P(("kv", "seq"), "exp", None),
    )
    out_specs = P(("kv", "seq"), None, "exp")
    return jax.shard_map(local, mesh=mesh, in_specs=in_specs, out_specs=out_specs, check_vma=False)
```
